512 devices in a mesh: src: 32 (over y_hi, z, core), cand: 16 (over x, y_lo).
Axes of the slice: x: 4, y: 8 (y_hi: 2, y_lo: 4; y = y_hi * 4 + y_lo), z: 8, core: 2. Of those that a mesh axis runs over, the one named last changes fastest.
Arguments:
- layer_input: bfloat16 [512, 128, 1024], P(('src', 'cand')), parts along dimension 0, may hold values from -16 to 16
- token_ids: int32 [512, 128], P(('src', 'cand')), parts along dimension 0, may hold values from 0 to 50264
- lengths: int32 [512], P(('src', 'cand')), parts along dimension 0, may hold values from 32 to 128
- idf_table: float32 [1608480], P('src'), parts along dimension 0, may hold values from 1 to 12
- query_weight: bfloat16 [1024, 1024], P('cand'), may hold values from -0.1875 to 0.1875
- key_weight: bfloat16 [1024, 1024], P('cand'), may hold values from -0.1875 to 0.1875
- value_weight: bfloat16 [1024, 1024], P('cand'), may hold values from -0.1875 to 0.1875
- output_weight: bfloat16 [1024, 1024], P('cand'), may hold values from -0.1875 to 0.1875
Outputs:
- embedded: bfloat16 [512, 128, 1024], P(('src', 'cand')), parts along dimension 0
- pair_utility: float32 [512, 16], P(('src', 'cand')), parts along dimension 0
- expected_utility: float32 [512], P(('src', 'cand')), parts along dimension 0
The draws below stay inside these ranges and needn't reach their ends.
There are 32 independent parts, one for each index of `src`. The reference program is written for one: setup_inputs(seed, part) draws one part's arguments, and reference() takes and returns one part's arrays. A program takes and returns all parts, laid end to end along the dimension named above; an argument that names none is the same for every part. Nothing has to cross between parts.
All inputs are finite; a program needn't handle non-finite values.
Results may differ from the reference program's by a relative error of at most 0.0086.
Values may be sent and summed in bfloat16 or wider, within the bound.
No kernel may reach another device: no remote copies, remote signals or barrier semaphores. Data moves between devices by JAX's collectives and lax.ppermute only.
A program may use at most 64 MiB of HBM per device.

```python
import math
import jax
import jax.numpy as jnp
import numpy as np
from jax import lax

D = 1024
HEADS = 16
HEAD = 64
VOCAB = 50265
L = 128
CANDS = 16


def draw_layer_input(key, part):
    base = jax.random.normal(jax.random.fold_in(key, 21), (L, D), jnp.float32)
    noise = jax.random.normal(key, (CANDS, L, D), jnp.float32)
    mixing = jax.random.uniform(jax.random.fold_in(key, 22), (CANDS, 1, 1), jnp.float32, 0.3, 0.9)
    offsets = jax.random.randint(jax.random.fold_in(key, 23), (CANDS, 1), 0, 4)
    positions = jnp.arange(L, dtype=jnp.int32)[None, :]
    source_rows = (positions + offsets) % L
    replaced = jax.random.randint(jax.random.fold_in(key, 24), (CANDS, L), 0, 10) == 0
    other_rows = jax.random.randint(jax.random.fold_in(key, 25), (CANDS, L), 0, L)
    source_rows = jnp.where(replaced, other_rows, source_rows).astype(jnp.int32)
    shared_rows = jnp.take(base, source_rows.reshape(CANDS * L), axis=0).reshape(CANDS, L, D)
    values = mixing * shared_rows + jnp.sqrt(1.0 - mixing * mixing) * noise
    values = jnp.clip(values, -4.0, 4.0)
    return values.astype(jnp.bfloat16)


def place_ends(result, key, low, top_value):
    extent = result.shape
    spot = [jax.random.randint(jax.random.fold_in(key, axis), (), 0, extent[axis]) for axis in range(len(extent))]
    result = result.at[tuple(spot)].set(low)
    longest = extent.index(max(extent))
    spot[longest] = (spot[longest] + 1) % extent[longest]
    return result.at[tuple(spot)].set(top_value)


def level_of(key, shape, shards, least, largest):
    def one(axis_at, shards_of):
        draws = jax.random.uniform(jax.random.fold_in(jax.random.fold_in(key, 6), axis_at), (shards_of,), jnp.float32, least / len(shards), largest / len(shards))
        return jnp.repeat(jnp.exp(draws), shape[axis_at] // shards_of).reshape((-1,) + (1,) * (len(shape) - axis_at - 1))

    gain = one(*shards[0])
    for cut in shards[1:]:
        gain = gain * one(*cut)
    return gain


def cumulative_ranks(amount, skew):
    portions = [(1 << 20) // math.isqrt(rank ** skew) + 1 for rank in range(1, amount + 1)]
    scale = 1 + sum(portions) // (1 << 30)
    return np.cumsum(np.array([max(1, weight // scale) for weight in portions]))


def ranked_ids(key, extent, count, skew):
    listing = cumulative_ranks(count, skew)
    lot = jax.random.randint(jax.random.fold_in(key, 1), extent, 0, int(listing[count - 1]))
    rank = jnp.searchsorted(jnp.asarray(listing, jnp.int32), lot, side="right")
    return jax.random.permutation(jax.random.fold_in(key, 2), count)[rank].astype(jnp.int32)


def gaussian(stream_key, extent, width, bound, shards=(), held_as=jnp.bfloat16):
    factor_of = level_of(stream_key, extent, shards, -0.22, 0.18) if shards else 1.0
    array = jax.random.normal(stream_key, extent, jnp.float32) * width * factor_of
    return jnp.minimum(jnp.maximum(array, -bound), bound).astype(held_as)


def setup_inputs(seed: int = 0, part: int = 0) -> dict:
    keys = jax.random.split(jax.random.key(seed), 9)
    part_keys = jax.random.split(jax.random.fold_in(keys[8], part), 9)
    return {
        "layer_input": draw_layer_input(jax.random.fold_in(jax.random.fold_in(keys[8], part), 71), part),
        "token_ids": place_ends(ranked_ids(part_keys[1], (CANDS, L), VOCAB, 2), jax.random.fold_in(part_keys[1], 3), 0, VOCAB - 1).astype(jnp.int32),
        "lengths": place_ends(jax.random.randint(part_keys[2], (CANDS,), L // 4, L + 1), jax.random.fold_in(part_keys[2], 1), L // 4, L).astype(jnp.int32),
        "idf_table": jnp.clip(jnp.exp(jax.random.uniform(part_keys[3], (VOCAB,), jnp.float32, math.log(1.0), math.log(12.0))), 1.0, 12.0),
        "query_weight": gaussian(keys[4], (D, D), D ** -0.5, 0.1875, ((0, 16),)),
        "key_weight": gaussian(keys[5], (D, D), D ** -0.5, 0.1875, ((0, 16),)),
        "value_weight": gaussian(keys[6], (D, D), D ** -0.5, 0.1875, ((0, 16),)),
        "output_weight": gaussian(keys[7], (D, D), D ** -0.5, 0.1875, ((0, 16),)),
    }


def encode(layer_input, lengths, query_weight, key_weight, value_weight, output_weight):
    flat = layer_input.reshape(CANDS * L, D)

    def project(weight):
        return jnp.dot(flat, weight, preferred_element_type=jnp.float32).astype(jnp.bfloat16)
    queries = project(query_weight).reshape(CANDS, L, HEADS, HEAD)
    key_rows = project(key_weight).reshape(CANDS, L, HEADS, HEAD)
    value_rows = project(value_weight).reshape(CANDS, L, HEADS, HEAD)
    positions = jnp.arange(L, dtype=jnp.int32)
    valid = positions[None, :] < lengths[:, None]
    scale = 1.0 / math.sqrt(HEAD)
    scores = jnp.einsum('clhe,cmhe->chlm', queries.astype(jnp.float32), key_rows.astype(jnp.float32), precision=lax.Precision.HIGHEST) * scale
    scores = jnp.where(valid[:, None, None, :], scores, -1000000000.0)
    highest = lax.optimization_barrier(jnp.max(scores, axis=-1, keepdims=True))
    expo = jnp.exp(scores - highest)
    probs = (expo / lax.optimization_barrier(jnp.sum(expo, axis=-1, keepdims=True))).astype(jnp.bfloat16)
    context = jnp.einsum('chlm,cmhe->clhe', probs.astype(jnp.float32), value_rows.astype(jnp.float32), precision=lax.Precision.HIGHEST).astype(jnp.bfloat16).reshape(CANDS * L, D)
    mixed = jnp.dot(context, output_weight, preferred_element_type=jnp.float32) + flat.astype(jnp.float32)
    centred = mixed - lax.optimization_barrier(jnp.mean(mixed, axis=-1, keepdims=True))
    squares = lax.optimization_barrier(jnp.sum(centred * centred, axis=-1, keepdims=True))
    embedded = (centred / jnp.sqrt(squares + 0.001)).astype(jnp.bfloat16)
    return (embedded.reshape(CANDS, L, D), valid)

def reference(layer_input, token_ids, lengths, idf_table, query_weight, key_weight, value_weight, output_weight):
    embedded, valid = encode(layer_input, lengths, query_weight, key_weight, value_weight, output_weight)
    token_weight = (jnp.take(idf_table, token_ids, axis=0) * valid.astype(jnp.float32)).astype(jnp.bfloat16)
    flat_vectors = embedded.reshape(CANDS * L, D).astype(jnp.float32)
    similarity = jnp.dot(flat_vectors, flat_vectors.T, precision=lax.Precision.HIGHEST).reshape(CANDS, L, CANDS, L)
    usable = token_weight > 0
    best_other = lax.optimization_barrier(jnp.max(jnp.where(usable[None, None, :, :], similarity, -4.0), axis=3))
    weight_float = token_weight.astype(jnp.float32)
    forward = jnp.einsum('il,ilj->ij', weight_float, best_other, precision=lax.Precision.HIGHEST)
    forward = forward / lax.optimization_barrier(jnp.sum(weight_float, axis=1))[:, None]
    pair_utility = 0.5 * (forward + forward.T)
    diagonal = jnp.diagonal(pair_utility)
    expected_utility = (lax.optimization_barrier(jnp.sum(pair_utility, axis=1)) - diagonal) / (CANDS - 1)
    return (embedded, pair_utility, expected_utility)
```

```python
import functools

import jax
import jax.numpy as jnp
import numpy as np
from jax import lax
from jax.experimental import pallas as pl
from jax.experimental.pallas import tpu as pltpu
from jax.sharding import Mesh, PartitionSpec as P

HEAD = 64
LANES = 128
PAD = 16
VMEM = pl.BlockSpec(memory_space=pltpu.VMEM)
SMEM = pl.BlockSpec(memory_space=pltpu.SMEM)


def params():
    return pltpu.CompilerParams(vmem_limit_bytes=40 * 1024 * 1024)


def prepare_kernel(lengths_ref, x_ref, q_ref, k_ref, v_ref, chunk_ref, ext_ref):
    core = lax.axis_index("core")
    rows = x_ref.shape[1]
    for block in range(4):
        at = pl.multiple_of(block * 2 * LANES + core * LANES, LANES)
        for n, ref in enumerate((q_ref, k_ref, v_ref)):
            piece = ref[:, pl.ds(at, LANES)]
            for y in range(4):
                chunk_ref[block * 4 + y, :, n * LANES : (n + 1) * LANES] = piece
    ext_ref[:rows, :] = x_ref[0]
    length = lengths_ref[0].astype(jnp.float32)
    ext_ref[rows:, :] = jnp.full((PAD, ext_ref.shape[1]), length, jnp.float32).astype(jnp.bfloat16)


def attend_kernel(x0, x1, x2, x3, wa_ref, wb_ref, o0, o1, o2, o3, part_ref, wo_ref):
    core = lax.axis_index("core")
    x = lax.axis_index("x")
    y = lax.axis_index("y")
    length = LANES
    for k, ref in enumerate((o0, o1, o2, o3)):
        at = pl.multiple_of(lax.rem(y + k, 4) * HEAD, HEAD)
        wo_ref[pl.ds(at, HEAD), :] = ref[...]
    xs = (x0, x1, x2, x3)
    tokens = jnp.concatenate([r[:length, :] for r in xs], axis=0)
    lane = lax.broadcasted_iota(jnp.int32, (length, LANES), 1)
    first = lane < HEAD
    lane2 = lax.broadcasted_iota(jnp.int32, (2 * length, length), 1).astype(jnp.float32)
    contexts = []
    for w_ref in (wa_ref, wb_ref):
        qkv = jnp.dot(tokens, w_ref[...], preferred_element_type=jnp.float32).astype(jnp.bfloat16)
        own = []
        for c in range(4):
            rows = slice(c * length, (c + 1) * length)
            q = qkv[rows, :LANES]
            key = qkv[rows, LANES : 2 * LANES]
            v = qkv[rows, 2 * LANES :]
            zero = jnp.zeros_like(q)
            both = jnp.concatenate([jnp.where(first, q, zero), jnp.where(first, zero, q)], axis=0)
            scores = lax.dot_general(
                both, key, (((1,), (1,)), ((), ())), preferred_element_type=jnp.float32
            ) * (HEAD ** -0.5)
            used = xs[c][length : length + 1, :length].astype(jnp.float32)
            scores = jnp.where(lane2 < used, scores, -1e9)
            expo = jnp.exp(scores - jnp.max(scores, axis=1, keepdims=True))
            probs = (expo / jnp.sum(expo, axis=1, keepdims=True)).astype(jnp.bfloat16)
            ctx = jnp.dot(probs, v, preferred_element_type=jnp.float32)
            own.append(jnp.where(first, ctx[:length], ctx[length:]).astype(jnp.bfloat16))
        contexts.append(jnp.concatenate(own, axis=0))
    wo_a = wo_ref[pl.ds(pl.multiple_of(core * LANES, LANES), LANES), :]
    wo_b = wo_ref[pl.ds(pl.multiple_of((1 - core) * LANES, LANES), LANES), :]
    part = jnp.dot(contexts[0], wo_a, preferred_element_type=jnp.float32)
    part = part + jnp.dot(contexts[1], wo_b, preferred_element_type=jnp.float32)
    for c in range(4):
        part_ref[lax.rem(x + c, 4)] = part[c * length : (c + 1) * length].astype(jnp.bfloat16)


def embed_kernel(weight_ref, parts_ref, x_ref, out_ref, ext_ref, row_ref):
    rows, width = x_ref.shape[1:]
    mixed = x_ref[0].astype(jnp.float32)
    for n in range(4):
        mixed = mixed + parts_ref[n].astype(jnp.float32)
    centred = mixed - jnp.mean(mixed, axis=1, keepdims=True)
    squares = jnp.sum(centred * centred, axis=1, keepdims=True)
    embedded = (centred / jnp.sqrt(squares + 0.001)).astype(jnp.bfloat16)
    out_ref[0] = embedded
    tail = jnp.concatenate(
        [jnp.broadcast_to(weight_ref[...].astype(jnp.float32), (PAD, LANES)), jnp.zeros((PAD, width - LANES), jnp.float32)],
        axis=1,
    ).astype(jnp.bfloat16)
    ext_ref[:rows, :] = embedded
    ext_ref[rows:, :] = tail
    for n in range(4):
        row_ref[n, :rows, :] = embedded
        row_ref[n, rows:, :] = tail


def pairs_kernel(row_ref, near_ref, far_ref, own_ref, out_ref):
    x = lax.axis_index("x")
    y = lax.axis_index("y")
    n = LANES
    me = x * 4 + y
    near = x * 4 + lax.rem(y + 1, 4)
    far = x * 4 + lax.rem(y + 2, 4)
    has_far = jnp.logical_or(y == 0, y == 3)
    rows = jnp.concatenate([row_ref[c, :n, :] for c in range(4)], axis=0)
    cols = jnp.concatenate([near_ref[:n, :], far_ref[:n, :], own_ref[:n, :]], axis=0)
    similar = lax.dot_general(rows, cols, (((1,), (1,)), ((), ())), preferred_element_type=jnp.float32)
    col_weight = [r[n : n + 1, :n].astype(jnp.float32) for r in (near_ref, far_ref, own_ref)]
    row_weight = [row_ref[c, n : n + 1, :n].astype(jnp.float32) for c in range(4)]
    down = [jnp.transpose(jnp.broadcast_to(w, (n, n))) for w in row_weight]
    row_sum = [jnp.sum(w, axis=1, keepdims=True) for w in row_weight]
    col_sum = [jnp.sum(w, axis=1, keepdims=True) for w in col_weight]
    col_sum[1] = jnp.where(has_far, col_sum[1], 1.0)
    dest = lax.broadcasted_iota(jnp.int32, (16, LANES), 0)
    lane = lax.broadcasted_iota(jnp.int32, (16, LANES), 1)
    total = jnp.zeros((16, LANES), jnp.float32)
    for j, other in enumerate((near, far, me)):
        w_col = col_weight[j]
        for c in range(4):
            block = similar[c * n : (c + 1) * n, j * n : (j + 1) * n]
            best_col = jnp.max(jnp.where(w_col > 0, block, -4.0), axis=1, keepdims=True)
            best_row = jnp.max(jnp.where(down[c] > 0, block, -4.0), axis=0, keepdims=True)
            forward = jnp.sum(best_col * down[c][:, :1], axis=0, keepdims=True) / row_sum[c]
            backward = jnp.sum(best_row * w_col, axis=1, keepdims=True) / col_sum[j]
            utility = 0.5 * (forward + backward)
            mate = c * 4 + y
            here = jnp.logical_and(dest == other, lane == mate)
            if j < 2:
                here = jnp.logical_or(here, jnp.logical_and(dest == mate, lane == other))
            if j == 1:
                here = jnp.logical_and(here, has_far)
            total = total + jnp.where(here, jnp.broadcast_to(utility, total.shape), 0.0)
    for p in range(16):
        out_ref[p] = jnp.broadcast_to(total[p : p + 1], (8, LANES))


def finish_kernel(got_ref, pair_ref, mean_ref):
    me = lax.axis_index("x") * 4 + lax.axis_index("y")
    total = got_ref[0]
    for p in range(1, 16):
        total = total + got_ref[p]
    lane = lax.broadcasted_iota(jnp.int32, total.shape, 1)
    pair_ref[...] = total[:1, :16]
    rest = jnp.where(jnp.logical_and(lane < 16, lane != me), total, 0.0)
    mean_ref[...] = (jnp.sum(rest, axis=1, keepdims=True) / 15)[:1]


def call(kernel, ins, outs, *args, scratch=()):
    return pl.pallas_call(
        kernel,
        in_specs=ins,
        out_specs=tuple(VMEM for _ in outs) if len(outs) > 1 else VMEM,
        out_shape=outs if len(outs) > 1 else outs[0],
        scratch_shapes=list(scratch),
        compiler_params=params(),
    )(*args)


def shift(size, by):
    return [((i + by) % size, i) for i in range(size)]


def shards(layer_input, token_ids, lengths, idf_table, query_weight, key_weight, value_weight, output_weight):
    _, length, width = layer_input.shape
    depth = query_weight.shape[0]
    bf16, f32 = jnp.bfloat16, jnp.float32
    chunks, extended = call(
        prepare_kernel,
        [SMEM] + [VMEM] * 4,
        (
            jax.ShapeDtypeStruct((16, depth, 3 * LANES), bf16),
            jax.ShapeDtypeStruct((length + PAD, width), bf16),
        ),
        lengths, layer_input, query_weight, key_weight, value_weight,
    )
    near_half = lax.all_to_all(chunks, ("x", "y"), split_axis=0, concat_axis=0, tiled=True)
    others = [lax.ppermute(extended, "x", shift(4, k)) for k in (1, 2, 3)]
    blocks = [lax.ppermute(output_weight, ("yh", "y"), shift(8, k)) for k in (1, 2, 7)]
    far_half = lax.ppermute(near_half, "core", [(0, 1), (1, 0)])
    parts = call(
        attend_kernel,
        [VMEM] * 10,
        (jax.ShapeDtypeStruct((4, length, width), bf16),),
        extended, *others,
        near_half.reshape(width, 3 * LANES), far_half.reshape(width, 3 * LANES),
        output_weight, *blocks,
        scratch=(pltpu.VMEM((4 * HEAD, width), bf16),),
    )
    parts = lax.all_to_all(parts, "x", split_axis=0, concat_axis=0, tiled=True)
    positions = jnp.arange(length, dtype=jnp.int32)
    valid = positions[None, :] < lengths[:, None]
    token_weight = (jnp.take(idf_table, token_ids, axis=0) * valid.astype(f32)).astype(bf16)
    embedded, own, row = call(
        embed_kernel,
        [VMEM] * 3,
        (
            jax.ShapeDtypeStruct((1, length, width), bf16),
            jax.ShapeDtypeStruct((length + PAD, width), bf16),
            jax.ShapeDtypeStruct((4, length + PAD, width), bf16),
        ),
        token_weight, parts, layer_input,
    )
    near = lax.ppermute(own, "y", shift(4, 1))
    far = lax.ppermute(own, "y", [(2, 0), (1, 3)])
    row = lax.all_to_all(row, "x", split_axis=0, concat_axis=0, tiled=True)
    known = call(
        pairs_kernel, [VMEM] * 4, (jax.ShapeDtypeStruct((16, 8, LANES), f32),), row, near, far, own
    )
    known = lax.all_to_all(known, ("x", "y"), split_axis=0, concat_axis=0, tiled=True)
    pair, mean = call(
        finish_kernel,
        [VMEM],
        (jax.ShapeDtypeStruct((1, 16), f32), jax.ShapeDtypeStruct((1, 1), f32)),
        known,
    )
    return embedded, pair, mean.reshape(1)


def solution(mesh):
    fine = Mesh(np.asarray(mesh.devices).reshape(2, 8, 2, 4, 4), ("yh", "z", "core", "x", "y"))
    src = ("yh", "z", "core")
    cand = ("x", "y")
    in_specs = (
        P(src + cand, None, None),
        P(src + cand, None),
        P(src + cand),
        P(src),
        P(cand, None),
        P(cand, None),
        P(cand, None),
        P(cand, None),
    )
    out_specs = (P(src + cand, None, None), P(src + cand, None), P(src + cand))
    return jax.shard_map(shards, mesh=fine, in_specs=in_specs, out_specs=out_specs, check_vma=False)
```

```python
import functools

import jax
import jax.numpy as jnp
import numpy as np
from jax import lax
from jax.experimental import pallas as pl
from jax.experimental.pallas import tpu as pltpu
from jax.sharding import Mesh, PartitionSpec as P

HEAD = 64
LANES = 128
PAD = 16
VMEM = pl.BlockSpec(memory_space=pltpu.VMEM)
SMEM = pl.BlockSpec(memory_space=pltpu.SMEM)


def params(mebibytes):
    return pltpu.CompilerParams(vmem_limit_bytes=mebibytes * 1024 * 1024)


def prepare_kernel(lengths_ref, x_hbm, q_hbm, k_hbm, v_hbm, chunk_ref, ext_ref, q_ref, k_ref, v_ref, sems):
    core = lax.axis_index("core")
    rows = x_hbm.shape[1]
    copies = [pltpu.make_async_copy(x_hbm.at[0], ext_ref.at[pl.ds(0, rows)], sems.at[3])]
    for n, (far, near) in enumerate(((q_hbm, q_ref), (k_hbm, k_ref), (v_hbm, v_ref))):
        copies.append(pltpu.make_async_copy(far, near, sems.at[n]))
    for copy in copies:
        copy.start()
    length = lengths_ref[0].astype(jnp.float32)
    ext_ref[rows:, :] = jnp.full((PAD, ext_ref.shape[1]), length, jnp.float32).astype(jnp.bfloat16)
    for n, ref in enumerate((q_ref, k_ref, v_ref)):
        copies[n + 1].wait()
        for block in range(4):
            at = pl.multiple_of(block * 2 * LANES + core * LANES, LANES)
            piece = ref[:, pl.ds(at, LANES)]
            for y in range(4):
                chunk_ref[block * 4 + y, :, n * LANES : (n + 1) * LANES] = piece
    copies[0].wait()


def attend_kernel(x0, x1, x2, x3, wa_ref, wb_ref, o0, o1, o2, o3, part_ref, wo_ref):
    core = lax.axis_index("core")
    x = lax.axis_index("x")
    y = lax.axis_index("y")
    length = LANES
    for k, ref in enumerate((o0, o1, o2, o3)):
        at = pl.multiple_of(lax.rem(y + k, 4) * HEAD, HEAD)
        wo_ref[pl.ds(at, HEAD), :] = ref[...]
    xs = (x0, x1, x2, x3)
    tokens = jnp.concatenate([r[:length, :] for r in xs], axis=0)
    lane = lax.broadcasted_iota(jnp.int32, (length, LANES), 1)
    first = lane < HEAD
    lane2 = lax.broadcasted_iota(jnp.int32, (2 * length, length), 1).astype(jnp.float32)
    contexts = []
    for w_ref in (wa_ref, wb_ref):
        qkv = jnp.dot(tokens, w_ref[...], preferred_element_type=jnp.float32).astype(jnp.bfloat16)
        own = []
        for c in range(4):
            rows = slice(c * length, (c + 1) * length)
            q = qkv[rows, :LANES]
            key = qkv[rows, LANES : 2 * LANES]
            v = qkv[rows, 2 * LANES :]
            zero = jnp.zeros_like(q)
            both = jnp.concatenate([jnp.where(first, q, zero), jnp.where(first, zero, q)], axis=0)
            scores = lax.dot_general(
                both, key, (((1,), (1,)), ((), ())), preferred_element_type=jnp.float32
            ) * (HEAD ** -0.5)
            used = xs[c][length : length + 1, :length].astype(jnp.float32)
            scores = jnp.where(lane2 < used, scores, -1e9)
            expo = jnp.exp(scores - jnp.max(scores, axis=1, keepdims=True))
            probs = (expo / jnp.sum(expo, axis=1, keepdims=True)).astype(jnp.bfloat16)
            ctx = jnp.dot(probs, v, preferred_element_type=jnp.float32)
            own.append(jnp.where(first, ctx[:length], ctx[length:]).astype(jnp.bfloat16))
        contexts.append(jnp.concatenate(own, axis=0))
    wo_a = wo_ref[pl.ds(pl.multiple_of(core * LANES, LANES), LANES), :]
    wo_b = wo_ref[pl.ds(pl.multiple_of((1 - core) * LANES, LANES), LANES), :]
    part = jnp.dot(contexts[0], wo_a, preferred_element_type=jnp.float32)
    part = part + jnp.dot(contexts[1], wo_b, preferred_element_type=jnp.float32)
    for c in range(4):
        part_ref[lax.rem(x + c, 4)] = part[c * length : (c + 1) * length].astype(jnp.bfloat16)


def embed_kernel(weight_ref, parts_ref, x_ref, out_ref, ext_ref, row_ref):
    rows, width = x_ref.shape[1:]
    mixed = x_ref[0].astype(jnp.float32)
    for n in range(4):
        mixed = mixed + parts_ref[n].astype(jnp.float32)
    centred = mixed - jnp.mean(mixed, axis=1, keepdims=True)
    squares = jnp.sum(centred * centred, axis=1, keepdims=True)
    embedded = (centred / jnp.sqrt(squares + 0.001)).astype(jnp.bfloat16)
    out_ref[0] = embedded
    tail = jnp.concatenate(
        [jnp.broadcast_to(weight_ref[...].astype(jnp.float32), (PAD, LANES)), jnp.zeros((PAD, width - LANES), jnp.float32)],
        axis=1,
    ).astype(jnp.bfloat16)
    ext_ref[:rows, :] = embedded
    ext_ref[rows:, :] = tail
    for n in range(4):
        row_ref[n, :rows, :] = embedded
        row_ref[n, rows:, :] = tail


def pairs_kernel(row_ref, near_ref, far_ref, own_ref, out_ref):
    x = lax.axis_index("x")
    y = lax.axis_index("y")
    n = LANES
    me = x * 4 + y
    near = x * 4 + lax.rem(y + 1, 4)
    far = x * 4 + lax.rem(y + 2, 4)
    has_far = jnp.logical_or(y == 0, y == 3)
    rows = jnp.concatenate([row_ref[c, :n, :] for c in range(4)], axis=0)
    cols = jnp.concatenate([near_ref[:n, :], far_ref[:n, :], own_ref[:n, :]], axis=0)
    similar = lax.dot_general(rows, cols, (((1,), (1,)), ((), ())), preferred_element_type=jnp.float32)
    col_weight = [r[n : n + 1, :n].astype(jnp.float32) for r in (near_ref, far_ref, own_ref)]
    row_weight = [row_ref[c, n : n + 1, :n].astype(jnp.float32) for c in range(4)]
    down = [jnp.transpose(jnp.broadcast_to(w, (n, n))) for w in row_weight]
    row_sum = [jnp.sum(w, axis=1, keepdims=True) for w in row_weight]
    col_sum = [jnp.sum(w, axis=1, keepdims=True) for w in col_weight]
    col_sum[1] = jnp.where(has_far, col_sum[1], 1.0)
    dest = lax.broadcasted_iota(jnp.int32, (16, LANES), 0)
    lane = lax.broadcasted_iota(jnp.int32, (16, LANES), 1)
    total = jnp.zeros((16, LANES), jnp.float32)
    for j, other in enumerate((near, far, me)):
        w_col = col_weight[j]
        for c in range(4):
            block = similar[c * n : (c + 1) * n, j * n : (j + 1) * n]
            best_col = jnp.max(jnp.where(w_col > 0, block, -4.0), axis=1, keepdims=True)
            best_row = jnp.max(jnp.where(down[c] > 0, block, -4.0), axis=0, keepdims=True)
            forward = jnp.sum(best_col * down[c][:, :1], axis=0, keepdims=True) / row_sum[c]
            backward = jnp.sum(best_row * w_col, axis=1, keepdims=True) / col_sum[j]
            utility = 0.5 * (forward + backward)
            mate = c * 4 + y
            here = jnp.logical_and(dest == other, lane == mate)
            if j < 2:
                here = jnp.logical_or(here, jnp.logical_and(dest == mate, lane == other))
            if j == 1:
                here = jnp.logical_and(here, has_far)
            total = total + jnp.where(here, jnp.broadcast_to(utility, total.shape), 0.0)
    for p in range(16):
        out_ref[p] = jnp.broadcast_to(total[p : p + 1], (8, LANES))


def finish_kernel(got_ref, pair_ref, mean_ref):
    me = lax.axis_index("x") * 4 + lax.axis_index("y")
    total = got_ref[0]
    for p in range(1, 16):
        total = total + got_ref[p]
    lane = lax.broadcasted_iota(jnp.int32, total.shape, 1)
    pair_ref[...] = total[:1, :16]
    rest = jnp.where(jnp.logical_and(lane < 16, lane != me), total, 0.0)
    mean_ref[...] = (jnp.sum(rest, axis=1, keepdims=True) / 15)[:1]


def call(kernel, ins, outs, *args, scratch=(), mebibytes=40):
    return pl.pallas_call(
        kernel,
        in_specs=ins,
        out_specs=tuple(VMEM for _ in outs) if len(outs) > 1 else VMEM,
        out_shape=outs if len(outs) > 1 else outs[0],
        scratch_shapes=list(scratch),
        compiler_params=params(mebibytes),
    )(*args)


def shift(size, by):
    return [((i + by) % size, i) for i in range(size)]


def shards(layer_input, token_ids, lengths, idf_table, query_weight, key_weight, value_weight, output_weight):
    _, length, width = layer_input.shape
    depth = query_weight.shape[0]
    bf16, f32 = jnp.bfloat16, jnp.float32
    chunks, extended = call(
        prepare_kernel,
        [SMEM] + [pl.BlockSpec(memory_space=pltpu.HBM)] * 4,
        (
            jax.ShapeDtypeStruct((16, depth, 3 * LANES), bf16),
            jax.ShapeDtypeStruct((length + PAD, width), bf16),
        ),
        lengths, layer_input, query_weight, key_weight, value_weight,
        scratch=[pltpu.VMEM((depth, width), bf16)] * 3 + [pltpu.SemaphoreType.DMA((4,))],
        mebibytes=63,
    )
    near_half = lax.all_to_all(chunks, ("x", "y"), split_axis=0, concat_axis=0, tiled=True)
    others = [lax.ppermute(extended, "x", shift(4, k)) for k in (1, 2, 3)]
    blocks = [lax.ppermute(output_weight, ("yh", "y"), shift(8, k)) for k in (1, 2, 7)]
    near_half, others, blocks = lax.optimization_barrier((near_half, others, blocks))
    far_half = lax.ppermute(near_half, "core", [(0, 1), (1, 0)])
    parts = call(
        attend_kernel,
        [VMEM] * 10,
        (jax.ShapeDtypeStruct((4, length, width), bf16),),
        extended, *others,
        near_half.reshape(width, 3 * LANES), far_half.reshape(width, 3 * LANES),
        output_weight, *blocks,
        scratch=(pltpu.VMEM((4 * HEAD, width), bf16),),
    )
    parts = lax.all_to_all(parts, "x", split_axis=0, concat_axis=0, tiled=True)
    positions = jnp.arange(length, dtype=jnp.int32)
    valid = positions[None, :] < lengths[:, None]
    token_weight = (jnp.take(idf_table, token_ids, axis=0) * valid.astype(f32)).astype(bf16)
    embedded, own, row = call(
        embed_kernel,
        [VMEM] * 3,
        (
            jax.ShapeDtypeStruct((1, length, width), bf16),
            jax.ShapeDtypeStruct((length + PAD, width), bf16),
            jax.ShapeDtypeStruct((4, length + PAD, width), bf16),
        ),
        token_weight, parts, layer_input,
    )
    near = lax.ppermute(own, "y", shift(4, 1))
    far = lax.ppermute(own, "y", [(2, 0), (1, 3)])
    row = lax.all_to_all(row, "x", split_axis=0, concat_axis=0, tiled=True)
    known = call(
        pairs_kernel, [VMEM] * 4, (jax.ShapeDtypeStruct((16, 8, LANES), f32),), row, near, far, own
    )
    known = lax.all_to_all(known, ("x", "y"), split_axis=0, concat_axis=0, tiled=True)
    pair, mean = call(
        finish_kernel,
        [VMEM],
        (jax.ShapeDtypeStruct((1, 16), f32), jax.ShapeDtypeStruct((1, 1), f32)),
        known,
    )
    return embedded, pair, mean.reshape(1)


def solution(mesh):
    fine = Mesh(np.asarray(mesh.devices).reshape(2, 8, 2, 4, 4), ("yh", "z", "core", "x", "y"))
    src = ("yh", "z", "core")
    cand = ("x", "y")
    in_specs = (
        P(src + cand, None, None),
        P(src + cand, None),
        P(src + cand),
        P(src),
        P(cand, None),
        P(cand, None),
        P(cand, None),
        P(cand, None),
    )
    out_specs = (P(src + cand, None, None), P(src + cand, None), P(src + cand))
    return jax.shard_map(shards, mesh=fine, in_specs=in_specs, out_specs=out_specs, check_vma=False)
```

```python
import functools

import jax
import jax.numpy as jnp
import numpy as np
from jax import lax
from jax.experimental import pallas as pl
from jax.experimental.pallas import tpu as pltpu
from jax.sharding import Mesh, PartitionSpec as P

HEAD = 64
LANES = 128
PAD = 16
VMEM = pl.BlockSpec(memory_space=pltpu.VMEM)
SMEM = pl.BlockSpec(memory_space=pltpu.SMEM)


def params(mebibytes):
    return pltpu.CompilerParams(vmem_limit_bytes=mebibytes * 1024 * 1024)


def prepare_kernel(lengths_ref, x_hbm, q_hbm, k_hbm, v_hbm, o_hbm, chunk_ref, ext_ref, q_ref, k_ref, v_ref, o_ref, sems):
    core = lax.axis_index("core")
    rows = x_hbm.shape[1]
    copies = [pltpu.make_async_copy(x_hbm.at[0], ext_ref.at[pl.ds(0, rows)], sems.at[4])]
    for n, (far, near) in enumerate(((q_hbm, q_ref), (k_hbm, k_ref), (v_hbm, v_ref), (o_hbm, o_ref))):
        copies.append(pltpu.make_async_copy(far, near, sems.at[n]))
    for copy in copies:
        copy.start()
    length = lengths_ref[0].astype(jnp.float32)
    ext_ref[rows:, :] = jnp.full((PAD, ext_ref.shape[1]), length, jnp.float32).astype(jnp.bfloat16)
    for n, ref in enumerate((q_ref, k_ref, v_ref)):
        copies[n + 1].wait()
        for block in range(4):
            at = pl.multiple_of(block * 2 * LANES + core * LANES, LANES)
            piece = ref[:, pl.ds(at, LANES)]
            for y in range(4):
                chunk_ref[block * 4 + y, :, n * LANES : (n + 1) * LANES] = piece
    copies[4].wait()
    half = o_ref.shape[1] // 2
    piece = o_ref[:, pl.ds(pl.multiple_of(core * half, half), half)]
    for p in range(16):
        chunk_ref[p, :, 3 * LANES :] = piece
    copies[0].wait()


def attend_kernel(x0, x1, x2, x3, wa_ref, wb_ref, weight_ref, out_ref):
    core = lax.axis_index("core")
    x = lax.axis_index("x")
    length = LANES
    xs = (x0, x1, x2, x3)
    tokens = jnp.concatenate([r[:length, :] for r in xs], axis=0)
    first = lax.broadcasted_iota(jnp.int32, (length, LANES), 1) < HEAD
    position = lax.broadcasted_iota(jnp.int32, (2 * length, length), 1).astype(jnp.float32)
    for half, w_ref in enumerate((wa_ref, wb_ref)):
        columns = pl.ds(pl.multiple_of((core if half == 0 else 1 - core) * LANES, LANES), LANES)
        qkv = jnp.dot(tokens, w_ref[:, : 3 * LANES], preferred_element_type=jnp.float32).astype(jnp.bfloat16)
        for c in range(4):
            rows = slice(c * length, (c + 1) * length)
            q = qkv[rows, :LANES]
            key = qkv[rows, LANES : 2 * LANES]
            v = qkv[rows, 2 * LANES :]
            zero = jnp.zeros_like(q)
            both = jnp.concatenate([jnp.where(first, q, zero), jnp.where(first, zero, q)], axis=0)
            scores = lax.dot_general(
                both, key, (((1,), (1,)), ((), ())), preferred_element_type=jnp.float32
            ) * (HEAD ** -0.5)
            used = xs[c][length : length + 1, :length].astype(jnp.float32)
            scores = jnp.where(position < used, scores, -1e9)
            expo = jnp.exp(scores - jnp.max(scores, axis=1, keepdims=True))
            probs = (expo / jnp.sum(expo, axis=1, keepdims=True)).astype(jnp.bfloat16)
            ctx = jnp.dot(probs, v, preferred_element_type=jnp.float32)
            at = pl.multiple_of(lax.rem(x + c, 4) * length, length)
            context = jnp.where(first, ctx[:length], ctx[length:]).astype(jnp.bfloat16)
            for p in range(4):
                out_ref[p, pl.ds(at, length), columns] = context
    weight = jnp.broadcast_to(weight_ref[...].astype(jnp.float32), (PAD, LANES))
    weight = jnp.concatenate([weight, weight], axis=1).astype(jnp.bfloat16)
    for p in range(4):
        out_ref[p, 4 * length :, :] = weight


def embed_kernel(ctxs_ref, x0, x1, x2, x3, wa_ref, wb_ref, out_ref, ext_ref, row_ref, weight_ref, ctx_ref, mixed_ref):
    core = lax.axis_index("core")
    x = lax.axis_index("x")
    length = LANES
    width = out_ref.shape[2]
    for c in range(4):
        at = pl.multiple_of(lax.rem(x + c, 4) * length, length)
        for g in range(4):
            columns = slice(g * 4 * HEAD, (g + 1) * 4 * HEAD)
            ctx_ref[c * length : (c + 1) * length, columns] = ctxs_ref[g, pl.ds(at, length), :]
    half = width // 2
    for side, w_ref in ((core, wa_ref), (1 - core, wb_ref)):
        columns = pl.ds(pl.multiple_of(side * half, half), half)
        mixed_ref[:, columns] = jnp.dot(ctx_ref[...], w_ref[:, 3 * LANES :], preferred_element_type=jnp.float32)
    for c, x_ref in enumerate((x0, x1, x2, x3)):
        rows = slice(c * length, (c + 1) * length)
        mixed = mixed_ref[rows, :] + x_ref[:length, :].astype(jnp.float32)
        centred = mixed - jnp.mean(mixed, axis=1, keepdims=True)
        squares = jnp.sum(centred * centred, axis=1, keepdims=True)
        embedded = (centred / jnp.sqrt(squares + 0.001)).astype(jnp.bfloat16)
        row_ref[rows, :] = embedded
        if c == 0:
            out_ref[0] = embedded
            ext_ref[:length, :] = embedded
    own = ctxs_ref[x, 4 * length :, :]
    ext_ref[length:, :] = jnp.concatenate([own] * (width // (4 * HEAD)), axis=1)
    for c in range(4):
        weight_ref[c * PAD : (c + 1) * PAD, :] = ctxs_ref[lax.rem(x + c, 4), 4 * length :, :LANES].astype(jnp.float32)


def pairs_kernel(row_ref, weight_ref, near_ref, far_ref, out_ref):
    x = lax.axis_index("x")
    y = lax.axis_index("y")
    n = LANES
    me = x * 4 + y
    near = x * 4 + lax.rem(y + 1, 4)
    far = x * 4 + lax.rem(y + 2, 4)
    has_far = jnp.logical_or(y == 0, y == 3)
    cols = jnp.concatenate([near_ref[:n, :], far_ref[:n, :], row_ref[:n, :]], axis=0)
    similar = lax.dot_general(row_ref[...], cols, (((1,), (1,)), ((), ())), preferred_element_type=jnp.float32)
    row_weight = [weight_ref[c * PAD : c * PAD + 1, :] for c in range(4)]
    col_weight = [r[n : n + 1, :n].astype(jnp.float32) for r in (near_ref, far_ref)] + [row_weight[0]]
    down = [jnp.transpose(jnp.broadcast_to(w, (n, n))) for w in row_weight]
    row_sum = [jnp.sum(w, axis=1, keepdims=True) for w in row_weight]
    col_sum = [jnp.sum(w, axis=1, keepdims=True) for w in col_weight]
    col_sum[1] = jnp.where(has_far, col_sum[1], 1.0)
    dest = lax.broadcasted_iota(jnp.int32, (16, LANES), 0)
    lane = lax.broadcasted_iota(jnp.int32, (16, LANES), 1)
    total = jnp.zeros((16, LANES), jnp.float32)
    for j, other in enumerate((near, far, me)):
        w_col = col_weight[j]
        for c in range(4):
            block = similar[c * n : (c + 1) * n, j * n : (j + 1) * n]
            best_col = jnp.max(jnp.where(w_col > 0, block, -4.0), axis=1, keepdims=True)
            best_row = jnp.max(jnp.where(down[c] > 0, block, -4.0), axis=0, keepdims=True)
            forward = jnp.sum(best_col * down[c][:, :1], axis=0, keepdims=True) / row_sum[c]
            backward = jnp.sum(best_row * w_col, axis=1, keepdims=True) / col_sum[j]
            utility = 0.5 * (forward + backward)
            mate = lax.rem(x + c, 4) * 4 + y
            here = jnp.logical_and(dest == other, lane == mate)
            if j < 2:
                here = jnp.logical_or(here, jnp.logical_and(dest == mate, lane == other))
            if j == 1:
                here = jnp.logical_and(here, has_far)
            total = total + jnp.where(here, jnp.broadcast_to(utility, total.shape), 0.0)
    for p in range(16):
        out_ref[p] = jnp.broadcast_to(total[p : p + 1], (8, LANES))


def finish_kernel(got_ref, pair_ref, mean_ref):
    me = lax.axis_index("x") * 4 + lax.axis_index("y")
    total = got_ref[0]
    for p in range(1, 16):
        total = total + got_ref[p]
    lane = lax.broadcasted_iota(jnp.int32, total.shape, 1)
    pair_ref[...] = total[:1, :16]
    rest = jnp.where(jnp.logical_and(lane < 16, lane != me), total, 0.0)
    mean_ref[...] = (jnp.sum(rest, axis=1, keepdims=True) / 15)[:1]


def call(kernel, ins, outs, *args, scratch=(), mebibytes=20):
    return pl.pallas_call(
        kernel,
        in_specs=ins,
        out_specs=tuple(VMEM for _ in outs) if len(outs) > 1 else VMEM,
        out_shape=outs if len(outs) > 1 else outs[0],
        scratch_shapes=list(scratch),
        compiler_params=params(mebibytes),
    )(*args)


def shift(size, by):
    return [((i + by) % size, i) for i in range(size)]


def windows():
    groups = []
    for z in range(8):
        for core in range(2):
            for run in range(2):
                start = 4 * run + 2 * core + z % 2
                ys = sorted(((start + i) % 8 for i in range(4)), key=lambda y: y % 4)
                groups.append(
                    [(((y // 4 * 8 + z) * 2 + core) * 4 + x) * 4 + y % 4 for x in range(4) for y in ys]
                )
    return groups


def spread(chunks):
    axes = ("yh", "z", "core", "x", "y")
    return lax.all_to_all(chunks, axes, split_axis=0, concat_axis=0, tiled=True, axis_index_groups=windows())


def shards(layer_input, token_ids, lengths, idf_table, query_weight, key_weight, value_weight, output_weight):
    _, length, width = layer_input.shape
    depth = query_weight.shape[0]
    half = width // 2
    bf16, f32 = jnp.bfloat16, jnp.float32
    chunks, extended = call(
        prepare_kernel,
        [SMEM] + [pl.BlockSpec(memory_space=pltpu.HBM)] * 5,
        (
            jax.ShapeDtypeStruct((16, depth, 3 * LANES + half), bf16),
            jax.ShapeDtypeStruct((length + PAD, width), bf16),
        ),
        lengths, layer_input, query_weight, key_weight, value_weight, output_weight,
        scratch=[pltpu.VMEM((depth, width), bf16)] * 4 + [pltpu.SemaphoreType.DMA((5,))],
        mebibytes=63,
    )
    weights = spread(chunks)
    others = [lax.ppermute(extended, "x", shift(4, k)) for k in (1, 2, 3)]
    positions = jnp.arange(length, dtype=jnp.int32)
    valid = positions[None, :] < lengths[:, None]
    token_weight = (jnp.take(idf_table, token_ids, axis=0) * valid.astype(f32)).astype(bf16)
    weights, others, token_weight = lax.optimization_barrier((weights, others, token_weight))
    near_half = weights.reshape(width, 3 * LANES + half)
    far_half = lax.ppermute(near_half, "core", [(0, 1), (1, 0)])
    contexts = call(
        attend_kernel,
        [VMEM] * 7,
        (jax.ShapeDtypeStruct((4, 4 * length + PAD, 4 * HEAD), bf16),),
        extended, *others, near_half, far_half, token_weight,
    )
    contexts = lax.all_to_all(contexts, "x", split_axis=0, concat_axis=0, tiled=True)
    embedded, own, row, weights = call(
        embed_kernel,
        [VMEM] * 7,
        (
            jax.ShapeDtypeStruct((1, length, width), bf16),
            jax.ShapeDtypeStruct((length + PAD, width), bf16),
            jax.ShapeDtypeStruct((4 * length, width), bf16),
            jax.ShapeDtypeStruct((4 * PAD, LANES), f32),
        ),
        contexts, extended, *others, near_half, far_half,
        scratch=(pltpu.VMEM((4 * length, width), bf16), pltpu.VMEM((4 * length, width), f32)),
    )
    near = lax.ppermute(own, "y", shift(4, 1))
    far = lax.ppermute(own, "y", [(2, 0), (1, 3)])
    known = call(
        pairs_kernel, [VMEM] * 4, (jax.ShapeDtypeStruct((16, 8, LANES), f32),), row, weights, near, far
    )
    known = lax.all_to_all(known, ("x", "y"), split_axis=0, concat_axis=0, tiled=True)
    pair, mean = call(
        finish_kernel,
        [VMEM],
        (jax.ShapeDtypeStruct((1, 16), f32), jax.ShapeDtypeStruct((1, 1), f32)),
        known,
    )
    return embedded, pair, mean.reshape(1)


def solution(mesh):
    fine = Mesh(np.asarray(mesh.devices).reshape(2, 8, 2, 4, 4), ("yh", "z", "core", "x", "y"))
    src = ("yh", "z", "core")
    cand = ("x", "y")
    in_specs = (
        P(src + cand, None, None),
        P(src + cand, None),
        P(src + cand),
        P(src),
        P(cand, None),
        P(cand, None),
        P(cand, None),
        P(cand, None),
    )
    out_specs = (P(src + cand, None, None), P(src + cand, None), P(src + cand))
    return jax.shard_map(shards, mesh=fine, in_specs=in_specs, out_specs=out_specs, check_vma=False)
```

```python
import functools

import jax
import jax.numpy as jnp
import numpy as np
from jax import lax
from jax.experimental import pallas as pl
from jax.experimental.pallas import tpu as pltpu
from jax.sharding import Mesh, PartitionSpec as P

HEAD = 64
LANES = 128
PAD = 16
VMEM = pl.BlockSpec(memory_space=pltpu.VMEM)
SMEM = pl.BlockSpec(memory_space=pltpu.SMEM)


def params(mebibytes):
    return pltpu.CompilerParams(vmem_limit_bytes=mebibytes * 1024 * 1024)


def chunks_kernel(q_hbm, k_hbm, v_hbm, chunk_hbm, q_ref, k_ref, v_ref, piece_ref, sems, out_sems):
    core = lax.axis_index("core")
    copies = []
    for n, (far, near) in enumerate(((q_hbm, q_ref), (k_hbm, k_ref), (v_hbm, v_ref))):
        copies.append(pltpu.make_async_copy(far, near, sems.at[n]))
    for copy in copies:
        copy.start()
    for copy in copies:
        copy.wait()
    sends = []
    for block in range(4):
        at = pl.multiple_of(block * 2 * LANES + core * LANES, LANES)
        for n, ref in enumerate((q_ref, k_ref, v_ref)):
            piece_ref[block, :, n * LANES : (n + 1) * LANES] = ref[:, pl.ds(at, LANES)]
        for y in range(4):
            p = block * 4 + y
            send = pltpu.make_async_copy(piece_ref.at[block], chunk_hbm.at[p], out_sems.at[p])
            send.start()
            sends.append(send)
    for send in sends:
        send.wait()


def extend_kernel(x_ref, used_ref, o_ref, ext_ref, half_ref):
    half = half_ref.shape[0]
    half_ref[...] = o_ref[pl.ds(pl.multiple_of(lax.axis_index("core") * half, half), half), :]
    rows = x_ref.shape[1]
    ext_ref[:rows, :] = x_ref[0]
    used = jnp.concatenate([used_ref[...]] * (ext_ref.shape[1] // LANES), axis=1)
    ext_ref[rows:, :] = jnp.broadcast_to(used, (PAD, ext_ref.shape[1])).astype(jnp.bfloat16)


def heads(tokens, used, w_ref):
    length = LANES
    first = lax.broadcasted_iota(jnp.int32, (length, LANES), 1) < HEAD
    position = lax.broadcasted_iota(jnp.int32, (2 * length, length), 1).astype(jnp.float32)
    qkv = jnp.dot(tokens, w_ref[...], preferred_element_type=jnp.float32).astype(jnp.bfloat16)
    out = []
    for c in range(4):
        rows = slice(c * length, (c + 1) * length)
        q = qkv[rows, :LANES]
        key = qkv[rows, LANES : 2 * LANES]
        v = qkv[rows, 2 * LANES :]
        zero = jnp.zeros_like(q)
        both = jnp.concatenate([jnp.where(first, q, zero), jnp.where(first, zero, q)], axis=0)
        scores = lax.dot_general(
            both, key, (((1,), (1,)), ((), ())), preferred_element_type=jnp.float32
        ) * (HEAD ** -0.5)
        scores = jnp.where(position < used[c], scores, -1e9)
        expo = jnp.exp(scores - jnp.max(scores, axis=1, keepdims=True))
        probs = (expo / jnp.sum(expo, axis=1, keepdims=True)).astype(jnp.bfloat16)
        ctx = jnp.dot(probs, v, preferred_element_type=jnp.float32)
        out.append(jnp.where(first, ctx[:length], ctx[length:]).astype(jnp.bfloat16))
    return out


def row_of(refs):
    length = LANES
    tokens = jnp.concatenate([r[:length, :] for r in refs], axis=0)
    return tokens, [r[length : length + 1, :length].astype(jnp.float32) for r in refs]


def near_kernel(x0, x1, x2, x3, w_ref, out_ref):
    tokens, used = row_of((x0, x1, x2, x3))
    for c, context in enumerate(heads(tokens, used, w_ref)):
        out_ref[c * LANES : (c + 1) * LANES, :] = context


def far_kernel(x0, x1, x2, x3, w_ref, near_ref, own_ref, mine_ref, mate_ref, part_ref, wo_ref):
    core = lax.axis_index("core")
    x = lax.axis_index("x")
    y = lax.axis_index("y")
    length = LANES
    half = HEAD // 2
    wo_ref[pl.ds(pl.multiple_of(y * HEAD, HEAD), HEAD), :] = own_ref[...]
    for side, ref in ((core, mine_ref), (1 - core, mate_ref)):
        at = pl.multiple_of(lax.rem(y + 1 + 2 * side, 4) * HEAD, HEAD)
        wo_ref[pl.ds(at, HEAD), :] = ref[:HEAD, :]
        at = pl.multiple_of(lax.rem(y + 2, 4) * HEAD + side * half, half)
        wo_ref[pl.ds(at, half), :] = ref[HEAD:, :]
    tokens, used = row_of((x0, x1, x2, x3))
    far = jnp.concatenate(heads(tokens, used, w_ref), axis=0)
    wo_a = wo_ref[pl.ds(pl.multiple_of(core * LANES, LANES), LANES), :]
    wo_b = wo_ref[pl.ds(pl.multiple_of((1 - core) * LANES, LANES), LANES), :]
    part = jnp.dot(near_ref[...], wo_a, preferred_element_type=jnp.float32)
    part = part + jnp.dot(far, wo_b, preferred_element_type=jnp.float32)
    for c in range(4):
        part_ref[lax.rem(x + c, 4)] = part[c * length : (c + 1) * length].astype(jnp.bfloat16)


def embed_kernel(weight_ref, parts_ref, x_ref, out_ref, ext_ref, row_ref):
    rows, width = x_ref.shape[1:]
    mixed = x_ref[0].astype(jnp.float32)
    for n in range(4):
        mixed = mixed + parts_ref[n].astype(jnp.float32)
    centred = mixed - jnp.mean(mixed, axis=1, keepdims=True)
    squares = jnp.sum(centred * centred, axis=1, keepdims=True)
    embedded = (centred / jnp.sqrt(squares + 0.001)).astype(jnp.bfloat16)
    out_ref[0] = embedded
    tail = jnp.concatenate(
        [jnp.broadcast_to(weight_ref[...].astype(jnp.float32), (PAD, LANES)), jnp.zeros((PAD, width - LANES), jnp.float32)],
        axis=1,
    ).astype(jnp.bfloat16)
    ext_ref[:rows, :] = embedded
    ext_ref[rows:, :] = tail
    for n in range(4):
        row_ref[n, :rows, :] = embedded
        row_ref[n, rows:, :] = tail


def pairs_kernel(row_ref, near_ref, far_ref, own_ref, out_ref):
    x = lax.axis_index("x")
    y = lax.axis_index("y")
    n = LANES
    me = x * 4 + y
    near = x * 4 + lax.rem(y + 1, 4)
    far = x * 4 + lax.rem(y + 2, 4)
    has_far = jnp.logical_or(y == 0, y == 3)
    rows = jnp.concatenate([row_ref[c, :n, :] for c in range(4)], axis=0)
    cols = jnp.concatenate([near_ref[:n, :], far_ref[:n, :], own_ref[:n, :]], axis=0)
    similar = lax.dot_general(rows, cols, (((1,), (1,)), ((), ())), preferred_element_type=jnp.float32)
    col_weight = [r[n : n + 1, :n].astype(jnp.float32) for r in (near_ref, far_ref, own_ref)]
    row_weight = [row_ref[c, n : n + 1, :n].astype(jnp.float32) for c in range(4)]
    down = [jnp.transpose(jnp.broadcast_to(w, (n, n))) for w in row_weight]
    row_sum = [jnp.sum(w, axis=1, keepdims=True) for w in row_weight]
    col_sum = [jnp.sum(w, axis=1, keepdims=True) for w in col_weight]
    col_sum[1] = jnp.where(has_far, col_sum[1], 1.0)
    dest = lax.broadcasted_iota(jnp.int32, (16, LANES), 0)
    lane = lax.broadcasted_iota(jnp.int32, (16, LANES), 1)
    total = jnp.zeros((16, LANES), jnp.float32)
    for j, other in enumerate((near, far, me)):
        w_col = col_weight[j]
        for c in range(4):
            block = similar[c * n : (c + 1) * n, j * n : (j + 1) * n]
            best_col = jnp.max(jnp.where(w_col > 0, block, -4.0), axis=1, keepdims=True)
            best_row = jnp.max(jnp.where(down[c] > 0, block, -4.0), axis=0, keepdims=True)
            forward = jnp.sum(best_col * down[c][:, :1], axis=0, keepdims=True) / row_sum[c]
            backward = jnp.sum(best_row * w_col, axis=1, keepdims=True) / col_sum[j]
            utility = 0.5 * (forward + backward)
            mate = c * 4 + y
            here = jnp.logical_and(dest == other, lane == mate)
            if j < 2:
                here = jnp.logical_or(here, jnp.logical_and(dest == mate, lane == other))
            if j == 1:
                here = jnp.logical_and(here, has_far)
            total = total + jnp.where(here, jnp.broadcast_to(utility, total.shape), 0.0)
    for p in range(16):
        out_ref[p] = jnp.broadcast_to(total[p : p + 1], (8, LANES))


def finish_kernel(got_ref, pair_ref, mean_ref):
    me = lax.axis_index("x") * 4 + lax.axis_index("y")
    total = got_ref[0]
    for p in range(1, 16):
        total = total + got_ref[p]
    lane = lax.broadcasted_iota(jnp.int32, total.shape, 1)
    pair_ref[...] = total[:1, :16]
    rest = jnp.where(jnp.logical_and(lane < 16, lane != me), total, 0.0)
    mean_ref[...] = (jnp.sum(rest, axis=1, keepdims=True) / 15)[:1]


def call(kernel, ins, outs, *args, scratch=(), mebibytes=20):
    return pl.pallas_call(
        kernel,
        in_specs=ins,
        out_specs=tuple(VMEM for _ in outs) if len(outs) > 1 else VMEM,
        out_shape=outs if len(outs) > 1 else outs[0],
        scratch_shapes=list(scratch),
        compiler_params=params(mebibytes),
    )(*args)


def shift(size, by):
    return [((i + by) % size, i) for i in range(size)]


def sideways():
    pairs = []
    for y in range(8):
        for core in range(2):
            source = (y + (1 if core == 0 else 7)) % 8
            pairs.append(((source // 4 * 2 + core) * 4 + source % 4, (y // 4 * 2 + core) * 4 + y % 4))
    return pairs


def windows():
    groups = []
    for z in range(8):
        for core in range(2):
            for run in range(2):
                start = 4 * run + 2 * core + z % 2
                ys = sorted(((start + i) % 8 for i in range(4)), key=lambda y: y % 4)
                groups.append(
                    [(((y // 4 * 8 + z) * 2 + core) * 4 + x) * 4 + y % 4 for x in range(4) for y in ys]
                )
    return groups


def spread(chunks):
    axes = ("yh", "z", "core", "x", "y")
    return lax.all_to_all(chunks, axes, split_axis=0, concat_axis=0, tiled=True, axis_index_groups=windows())


def shards(layer_input, token_ids, lengths, idf_table, query_weight, key_weight, value_weight, output_weight):
    _, length, width = layer_input.shape
    depth = query_weight.shape[0]
    bf16, f32 = jnp.bfloat16, jnp.float32
    hbm = pl.BlockSpec(memory_space=pltpu.HBM)
    chunks = pl.pallas_call(
        chunks_kernel,
        in_specs=[hbm] * 3,
        out_specs=hbm,
        out_shape=jax.ShapeDtypeStruct((16, depth, 3 * LANES), bf16),
        scratch_shapes=[pltpu.VMEM((depth, width), bf16)] * 3
        + [
            pltpu.VMEM((4, depth, 3 * LANES), bf16),
            pltpu.SemaphoreType.DMA((3,)),
            pltpu.SemaphoreType.DMA((16,)),
        ],
        compiler_params=params(63),
    )(query_weight, key_weight, value_weight)
    used = jnp.broadcast_to(lengths.astype(f32)[:, None], (1, LANES))
    extended, half = call(
        extend_kernel,
        [VMEM] * 3,
        (jax.ShapeDtypeStruct((length + PAD, width), bf16), jax.ShapeDtypeStruct((depth // 2, width), bf16)),
        layer_input, used, output_weight,
    )
    beside = lax.ppermute(output_weight, ("yh", "core", "y"), sideways())
    across = lax.ppermute(half, ("yh", "y"), shift(8, 2))
    weights = spread(chunks)
    others = [lax.ppermute(extended, "x", shift(4, k)) for k in (1, 2, 3)]
    mine = jnp.concatenate([beside, across], axis=0)
    positions = jnp.arange(length, dtype=jnp.int32)
    valid = positions[None, :] < lengths[:, None]
    token_weight = (jnp.take(idf_table, token_ids, axis=0) * valid.astype(f32)).astype(bf16)
    weights, others, token_weight, mine = lax.optimization_barrier((weights, others, token_weight, mine))
    near_half = weights.reshape(width, 3 * LANES)
    far_half = lax.ppermute(near_half, "core", [(0, 1), (1, 0)])
    mate = lax.ppermute(mine, "core", [(0, 1), (1, 0)])
    context = call(
        near_kernel, [VMEM] * 5, (jax.ShapeDtypeStruct((4 * length, 2 * HEAD), bf16),), extended, *others, near_half
    )
    parts = call(
        far_kernel,
        [VMEM] * 9,
        (jax.ShapeDtypeStruct((4, length, width), bf16),),
        extended, *others, far_half, context, output_weight, mine, mate,
        scratch=(pltpu.VMEM((4 * HEAD, width), bf16),),
    )
    parts = lax.all_to_all(parts, "x", split_axis=0, concat_axis=0, tiled=True)
    embedded, own, row = call(
        embed_kernel,
        [VMEM] * 3,
        (
            jax.ShapeDtypeStruct((1, length, width), bf16),
            jax.ShapeDtypeStruct((length + PAD, width), bf16),
            jax.ShapeDtypeStruct((4, length + PAD, width), bf16),
        ),
        token_weight, parts, layer_input,
    )
    near = lax.ppermute(own, "y", shift(4, 1))
    far = lax.ppermute(own, "y", [(2, 0), (1, 3)])
    row = lax.all_to_all(row, "x", split_axis=0, concat_axis=0, tiled=True)
    known = call(
        pairs_kernel, [VMEM] * 4, (jax.ShapeDtypeStruct((16, 8, LANES), f32),), row, near, far, own
    )
    known = lax.all_to_all(known, ("x", "y"), split_axis=0, concat_axis=0, tiled=True)
    pair, mean = call(
        finish_kernel,
        [VMEM],
        (jax.ShapeDtypeStruct((1, 16), f32), jax.ShapeDtypeStruct((1, 1), f32)),
        known,
    )
    return embedded, pair, mean.reshape(1)


def solution(mesh):
    fine = Mesh(np.asarray(mesh.devices).reshape(2, 8, 2, 4, 4), ("yh", "z", "core", "x", "y"))
    src = ("yh", "z", "core")
    cand = ("x", "y")
    in_specs = (
        P(src + cand, None, None),
        P(src + cand, None),
        P(src + cand),
        P(src),
        P(cand, None),
        P(cand, None),
        P(cand, None),
        P(cand, None),
    )
    out_specs = (P(src + cand, None, None), P(src + cand, None), P(src + cand))
    return jax.shard_map(shards, mesh=fine, in_specs=in_specs, out_specs=out_specs, check_vma=False)
```

```python
import functools

import jax
import jax.numpy as jnp
import numpy as np
from jax import lax
from jax.experimental import pallas as pl
from jax.experimental.pallas import tpu as pltpu
from jax.sharding import Mesh, PartitionSpec as P

HEAD = 64
LANES = 128
PAD = 16
VMEM = pl.BlockSpec(memory_space=pltpu.VMEM)
SMEM = pl.BlockSpec(memory_space=pltpu.SMEM)


def params(mebibytes):
    return pltpu.CompilerParams(vmem_limit_bytes=mebibytes * 1024 * 1024)


def chunks_kernel(q_hbm, k_hbm, v_hbm, chunk_hbm, q_ref, k_ref, v_ref, piece_ref, sems, out_sems):
    core = lax.axis_index("core")
    copies = []
    for n, (far, near) in enumerate(((q_hbm, q_ref), (k_hbm, k_ref), (v_hbm, v_ref))):
        copies.append(pltpu.make_async_copy(far, near, sems.at[n]))
    for copy in copies:
        copy.start()
    for copy in copies:
        copy.wait()
    sends = []
    for block in range(4):
        at = pl.multiple_of(block * 2 * LANES + core * LANES, LANES)
        for n, ref in enumerate((q_ref, k_ref, v_ref)):
            piece_ref[block, :, n * LANES : (n + 1) * LANES] = ref[:, pl.ds(at, LANES)]
        for y in range(4):
            p = block * 4 + y
            send = pltpu.make_async_copy(piece_ref.at[block], chunk_hbm.at[p], out_sems.at[p])
            send.start()
            sends.append(send)
    for send in sends:
        send.wait()


def extend_kernel(x_ref, used_ref, o_ref, ext_ref, half_ref, block_ref):
    half = half_ref.shape[0]
    block_ref[...] = o_ref[...]
    half_ref[...] = o_ref[pl.ds(pl.multiple_of(lax.axis_index("core") * half, half), half), :]
    rows = x_ref.shape[1]
    ext_ref[:rows, :] = x_ref[0]
    used = jnp.concatenate([used_ref[...]] * (ext_ref.shape[1] // LANES), axis=1)
    ext_ref[rows:, :] = jnp.broadcast_to(used, (PAD, ext_ref.shape[1])).astype(jnp.bfloat16)


def heads(tokens, used, w_ref):
    length = LANES
    first = lax.broadcasted_iota(jnp.int32, (length, LANES), 1) < HEAD
    position = lax.broadcasted_iota(jnp.int32, (2 * length, length), 1).astype(jnp.float32)
    qkv = jnp.dot(tokens, w_ref[...], preferred_element_type=jnp.float32).astype(jnp.bfloat16)
    out = []
    for c in range(4):
        rows = slice(c * length, (c + 1) * length)
        q = qkv[rows, :LANES]
        key = qkv[rows, LANES : 2 * LANES]
        v = qkv[rows, 2 * LANES :]
        zero = jnp.zeros_like(q)
        both = jnp.concatenate([jnp.where(first, q, zero), jnp.where(first, zero, q)], axis=0)
        scores = lax.dot_general(
            both, key, (((1,), (1,)), ((), ())), preferred_element_type=jnp.float32
        ) * (HEAD ** -0.5)
        scores = jnp.where(position < used[c], scores, -1e9)
        expo = jnp.exp(scores - jnp.max(scores, axis=1, keepdims=True))
        probs = (expo / jnp.sum(expo, axis=1, keepdims=True)).astype(jnp.bfloat16)
        ctx = jnp.dot(probs, v, preferred_element_type=jnp.float32)
        out.append(jnp.where(first, ctx[:length], ctx[length:]).astype(jnp.bfloat16))
    return out


def row_of(refs):
    length = LANES
    tokens = jnp.concatenate([r[:length, :] for r in refs], axis=0)
    return tokens, [r[length : length + 1, :length].astype(jnp.float32) for r in refs]


def near_kernel(x0, x1, x2, x3, w_ref, out_ref):
    tokens, used = row_of((x0, x1, x2, x3))
    for c, context in enumerate(heads(tokens, used, w_ref)):
        out_ref[c * LANES : (c + 1) * LANES, :] = context


def far_kernel(x0, x1, x2, x3, w_ref, near_ref, own_ref, mine_ref, mate_ref, part_ref, wo_ref):
    core = lax.axis_index("core")
    x = lax.axis_index("x")
    y = lax.axis_index("y")
    length = LANES
    half = HEAD // 2
    wo_ref[pl.ds(pl.multiple_of(y * HEAD, HEAD), HEAD), :] = own_ref[...]
    for side, ref in ((core, mine_ref), (1 - core, mate_ref)):
        at = pl.multiple_of(lax.rem(y + 1 + 2 * side, 4) * HEAD, HEAD)
        wo_ref[pl.ds(at, HEAD), :] = ref[:HEAD, :]
        at = pl.multiple_of(lax.rem(y + 2, 4) * HEAD + side * half, half)
        wo_ref[pl.ds(at, half), :] = ref[HEAD:, :]
    tokens, used = row_of((x0, x1, x2, x3))
    far = jnp.concatenate(heads(tokens, used, w_ref), axis=0)
    wo_a = wo_ref[pl.ds(pl.multiple_of(core * LANES, LANES), LANES), :]
    wo_b = wo_ref[pl.ds(pl.multiple_of((1 - core) * LANES, LANES), LANES), :]
    part = jnp.dot(near_ref[...], wo_a, preferred_element_type=jnp.float32)
    part = part + jnp.dot(far, wo_b, preferred_element_type=jnp.float32)
    for c in range(4):
        part_ref[lax.rem(x + c, 4)] = part[c * length : (c + 1) * length].astype(jnp.bfloat16)


def embed_kernel(weight_ref, parts_ref, x_ref, out_ref, ext_ref, row_ref):
    rows, width = x_ref.shape[1:]
    mixed = x_ref[0].astype(jnp.float32)
    for n in range(4):
        mixed = mixed + parts_ref[n].astype(jnp.float32)
    centred = mixed - jnp.mean(mixed, axis=1, keepdims=True)
    squares = jnp.sum(centred * centred, axis=1, keepdims=True)
    embedded = (centred / jnp.sqrt(squares + 0.001)).astype(jnp.bfloat16)
    out_ref[0] = embedded
    tail = jnp.concatenate(
        [jnp.broadcast_to(weight_ref[...].astype(jnp.float32), (PAD, LANES)), jnp.zeros((PAD, width - LANES), jnp.float32)],
        axis=1,
    ).astype(jnp.bfloat16)
    ext_ref[:rows, :] = embedded
    ext_ref[rows:, :] = tail
    for n in range(4):
        row_ref[n, :rows, :] = embedded
        row_ref[n, rows:, :] = tail


def pairs_kernel(row_ref, near_ref, far_ref, own_ref, out_ref):
    x = lax.axis_index("x")
    y = lax.axis_index("y")
    n = LANES
    me = x * 4 + y
    near = x * 4 + lax.rem(y + 1, 4)
    far = x * 4 + lax.rem(y + 2, 4)
    has_far = jnp.logical_or(y == 0, y == 3)
    rows = jnp.concatenate([row_ref[c, :n, :] for c in range(4)], axis=0)
    cols = jnp.concatenate([near_ref[:n, :], far_ref[:n, :], own_ref[:n, :]], axis=0)
    similar = lax.dot_general(rows, cols, (((1,), (1,)), ((), ())), preferred_element_type=jnp.float32)
    col_weight = [r[n : n + 1, :n].astype(jnp.float32) for r in (near_ref, far_ref, own_ref)]
    row_weight = [row_ref[c, n : n + 1, :n].astype(jnp.float32) for c in range(4)]
    down = [jnp.transpose(jnp.broadcast_to(w, (n, n))) for w in row_weight]
    row_sum = [jnp.sum(w, axis=1, keepdims=True) for w in row_weight]
    col_sum = [jnp.sum(w, axis=1, keepdims=True) for w in col_weight]
    col_sum[1] = jnp.where(has_far, col_sum[1], 1.0)
    dest = lax.broadcasted_iota(jnp.int32, (16, LANES), 0)
    lane = lax.broadcasted_iota(jnp.int32, (16, LANES), 1)
    total = jnp.zeros((16, LANES), jnp.float32)
    for j, other in enumerate((near, far, me)):
        w_col = col_weight[j]
        for c in range(4):
            block = similar[c * n : (c + 1) * n, j * n : (j + 1) * n]
            best_col = jnp.max(jnp.where(w_col > 0, block, -4.0), axis=1, keepdims=True)
            best_row = jnp.max(jnp.where(down[c] > 0, block, -4.0), axis=0, keepdims=True)
            forward = jnp.sum(best_col * down[c][:, :1], axis=0, keepdims=True) / row_sum[c]
            backward = jnp.sum(best_row * w_col, axis=1, keepdims=True) / col_sum[j]
            utility = 0.5 * (forward + backward)
            mate = c * 4 + y
            here = jnp.logical_and(dest == other, lane == mate)
            if j < 2:
                here = jnp.logical_or(here, jnp.logical_and(dest == mate, lane == other))
            if j == 1:
                here = jnp.logical_and(here, has_far)
            total = total + jnp.where(here, jnp.broadcast_to(utility, total.shape), 0.0)
    for p in range(16):
        out_ref[p] = jnp.broadcast_to(total[p : p + 1], (8, LANES))


def finish_kernel(got_ref, pair_ref, mean_ref):
    me = lax.axis_index("x") * 4 + lax.axis_index("y")
    total = got_ref[0]
    for p in range(1, 16):
        total = total + got_ref[p]
    lane = lax.broadcasted_iota(jnp.int32, total.shape, 1)
    pair_ref[...] = total[:1, :16]
    rest = jnp.where(jnp.logical_and(lane < 16, lane != me), total, 0.0)
    mean_ref[...] = (jnp.sum(rest, axis=1, keepdims=True) / 15)[:1]


def call(kernel, ins, outs, *args, scratch=(), mebibytes=20):
    return pl.pallas_call(
        kernel,
        in_specs=ins,
        out_specs=tuple(VMEM for _ in outs) if len(outs) > 1 else VMEM,
        out_shape=outs if len(outs) > 1 else outs[0],
        scratch_shapes=list(scratch),
        compiler_params=params(mebibytes),
    )(*args)


def shift(size, by):
    return [((i + by) % size, i) for i in range(size)]


def sideways():
    pairs = []
    for y in range(8):
        for core in range(2):
            source = (y + (1 if core == 0 else 7)) % 8
            pairs.append(((source // 4 * 2 + core) * 4 + source % 4, (y // 4 * 2 + core) * 4 + y % 4))
    return pairs


def windows():
    groups = []
    for z in range(8):
        for core in range(2):
            for run in range(2):
                start = 4 * run + 2 * core + z % 2
                ys = sorted(((start + i) % 8 for i in range(4)), key=lambda y: y % 4)
                groups.append(
                    [(((y // 4 * 8 + z) * 2 + core) * 4 + x) * 4 + y % 4 for x in range(4) for y in ys]
                )
    return groups


def spread(chunks):
    axes = ("yh", "z", "core", "x", "y")
    return lax.all_to_all(chunks, axes, split_axis=0, concat_axis=0, tiled=True, axis_index_groups=windows())


def shards(layer_input, token_ids, lengths, idf_table, query_weight, key_weight, value_weight, output_weight):
    _, length, width = layer_input.shape
    depth = query_weight.shape[0]
    bf16, f32 = jnp.bfloat16, jnp.float32
    hbm = pl.BlockSpec(memory_space=pltpu.HBM)
    chunks = pl.pallas_call(
        chunks_kernel,
        in_specs=[hbm] * 3,
        out_specs=hbm,
        out_shape=jax.ShapeDtypeStruct((16, depth, 3 * LANES), bf16),
        scratch_shapes=[pltpu.VMEM((depth, width), bf16)] * 3
        + [
            pltpu.VMEM((4, depth, 3 * LANES), bf16),
            pltpu.SemaphoreType.DMA((3,)),
            pltpu.SemaphoreType.DMA((16,)),
        ],
        compiler_params=params(63),
    )(query_weight, key_weight, value_weight)
    used = jnp.broadcast_to(lengths.astype(f32)[:, None], (1, LANES))
    extended, half, block = call(
        extend_kernel,
        [VMEM] * 3,
        (
            jax.ShapeDtypeStruct((length + PAD, width), bf16),
            jax.ShapeDtypeStruct((depth // 2, width), bf16),
            jax.ShapeDtypeStruct((depth, width), bf16),
        ),
        layer_input, used, output_weight,
    )
    beside = lax.ppermute(block, ("yh", "core", "y"), sideways())
    across = lax.ppermute(half, ("yh", "y"), shift(8, 2))
    weights = spread(chunks)
    others = [lax.ppermute(extended, "x", shift(4, k)) for k in (1, 2, 3)]
    mine = jnp.concatenate([beside, across], axis=0)
    positions = jnp.arange(length, dtype=jnp.int32)
    valid = positions[None, :] < lengths[:, None]
    token_weight = (jnp.take(idf_table, token_ids, axis=0) * valid.astype(f32)).astype(bf16)
    weights, others, token_weight, mine = lax.optimization_barrier((weights, others, token_weight, mine))
    near_half = weights.reshape(width, 3 * LANES)
    far_half = lax.ppermute(near_half, "core", [(0, 1), (1, 0)])
    mate = lax.ppermute(mine, "core", [(0, 1), (1, 0)])
    context = call(
        near_kernel, [VMEM] * 5, (jax.ShapeDtypeStruct((4 * length, 2 * HEAD), bf16),), extended, *others, near_half
    )
    parts = call(
        far_kernel,
        [VMEM] * 9,
        (jax.ShapeDtypeStruct((4, length, width), bf16),),
        extended, *others, far_half, context, output_weight, mine, mate,
        scratch=(pltpu.VMEM((4 * HEAD, width), bf16),),
    )
    parts = lax.all_to_all(parts, "x", split_axis=0, concat_axis=0, tiled=True)
    embedded, own, row = call(
        embed_kernel,
        [VMEM] * 3,
        (
            jax.ShapeDtypeStruct((1, length, width), bf16),
            jax.ShapeDtypeStruct((length + PAD, width), bf16),
            jax.ShapeDtypeStruct((4, length + PAD, width), bf16),
        ),
        token_weight, parts, layer_input,
    )
    near = lax.ppermute(own, "y", shift(4, 1))
    far = lax.ppermute(own, "y", [(2, 0), (1, 3)])
    row = lax.all_to_all(row, "x", split_axis=0, concat_axis=0, tiled=True)
    known = call(
        pairs_kernel, [VMEM] * 4, (jax.ShapeDtypeStruct((16, 8, LANES), f32),), row, near, far, own
    )
    known = lax.all_to_all(known, ("x", "y"), split_axis=0, concat_axis=0, tiled=True)
    pair, mean = call(
        finish_kernel,
        [VMEM],
        (jax.ShapeDtypeStruct((1, 16), f32), jax.ShapeDtypeStruct((1, 1), f32)),
        known,
    )
    return embedded, pair, mean.reshape(1)


def solution(mesh):
    fine = Mesh(np.asarray(mesh.devices).reshape(2, 8, 2, 4, 4), ("yh", "z", "core", "x", "y"))
    src = ("yh", "z", "core")
    cand = ("x", "y")
    in_specs = (
        P(src + cand, None, None),
        P(src + cand, None),
        P(src + cand),
        P(src),
        P(cand, None),
        P(cand, None),
        P(cand, None),
        P(cand, None),
    )
    out_specs = (P(src + cand, None, None), P(src + cand, None), P(src + cand))
    return jax.shard_map(shards, mesh=fine, in_specs=in_specs, out_specs=out_specs, check_vma=False)
```

```python
import functools

import jax
import jax.numpy as jnp
import numpy as np
from jax import lax
from jax.experimental import pallas as pl
from jax.experimental.pallas import tpu as pltpu
from jax.sharding import Mesh, PartitionSpec as P

HEAD = 64
LANES = 128
PAD = 16
VMEM = pl.BlockSpec(memory_space=pltpu.VMEM)
SMEM = pl.BlockSpec(memory_space=pltpu.SMEM)


def params(mebibytes):
    return pltpu.CompilerParams(vmem_limit_bytes=mebibytes * 1024 * 1024)


def chunks_kernel(q_hbm, k_hbm, v_hbm, chunk_hbm, piece_ref, sems, out_sems):
    core = lax.axis_index("core")
    copies = []
    for block in range(4):
        at = pl.multiple_of(block * 2 * LANES + core * LANES, LANES)
        for n, ref in enumerate((q_hbm, k_hbm, v_hbm)):
            to = piece_ref.at[block, :, pl.ds(n * LANES, LANES)]
            copies.append(pltpu.make_async_copy(ref.at[:, pl.ds(at, LANES)], to, sems.at[block * 3 + n]))
    for copy in copies:
        copy.start()
    sends = []
    for block in range(4):
        for n in range(3):
            copies[block * 3 + n].wait()
        for y in range(4):
            p = block * 4 + y
            send = pltpu.make_async_copy(piece_ref.at[block], chunk_hbm.at[p], out_sems.at[p])
            send.start()
            sends.append(send)
    for send in sends:
        send.wait()


def extend_kernel(x_ref, used_ref, o_ref, ext_ref, half_ref, block_ref):
    half = half_ref.shape[0]
    block_ref[...] = o_ref[...]
    half_ref[...] = o_ref[pl.ds(pl.multiple_of(lax.axis_index("core") * half, half), half), :]
    rows = x_ref.shape[1]
    ext_ref[:rows, :] = x_ref[0]
    used = jnp.concatenate([used_ref[...]] * (ext_ref.shape[1] // LANES), axis=1)
    ext_ref[rows:, :] = jnp.broadcast_to(used, (PAD, ext_ref.shape[1])).astype(jnp.bfloat16)


def heads(tokens, used, w_ref):
    length = LANES
    first = lax.broadcasted_iota(jnp.int32, (length, LANES), 1) < HEAD
    position = lax.broadcasted_iota(jnp.int32, (2 * length, length), 1).astype(jnp.float32)
    qkv = jnp.dot(tokens, w_ref[...], preferred_element_type=jnp.float32).astype(jnp.bfloat16)
    out = []
    for c in range(4):
        rows = slice(c * length, (c + 1) * length)
        q = qkv[rows, :LANES]
        key = qkv[rows, LANES : 2 * LANES]
        v = qkv[rows, 2 * LANES :]
        zero = jnp.zeros_like(q)
        both = jnp.concatenate([jnp.where(first, q, zero), jnp.where(first, zero, q)], axis=0)
        scores = lax.dot_general(
            both, key, (((1,), (1,)), ((), ())), preferred_element_type=jnp.float32
        ) * (HEAD ** -0.5)
        scores = jnp.where(position < used[c], scores, -1e9)
        expo = jnp.exp(scores - jnp.max(scores, axis=1, keepdims=True))
        probs = (expo / jnp.sum(expo, axis=1, keepdims=True)).astype(jnp.bfloat16)
        ctx = jnp.dot(probs, v, preferred_element_type=jnp.float32)
        out.append(jnp.where(first, ctx[:length], ctx[length:]).astype(jnp.bfloat16))
    return out


def row_of(refs):
    length = LANES
    tokens = jnp.concatenate([r[:length, :] for r in refs], axis=0)
    return tokens, [r[length : length + 1, :length].astype(jnp.float32) for r in refs]


def near_kernel(x0, x1, x2, x3, w_ref, out_ref):
    tokens, used = row_of((x0, x1, x2, x3))
    for c, context in enumerate(heads(tokens, used, w_ref)):
        out_ref[c * LANES : (c + 1) * LANES, :] = context


def far_kernel(x0, x1, x2, x3, w_ref, near_ref, own_ref, mine_ref, mate_ref, part_ref, wo_ref):
    core = lax.axis_index("core")
    x = lax.axis_index("x")
    y = lax.axis_index("y")
    length = LANES
    half = HEAD // 2
    wo_ref[pl.ds(pl.multiple_of(y * HEAD, HEAD), HEAD), :] = own_ref[...]
    for side, ref in ((core, mine_ref), (1 - core, mate_ref)):
        at = pl.multiple_of(lax.rem(y + 1 + 2 * side, 4) * HEAD, HEAD)
        wo_ref[pl.ds(at, HEAD), :] = ref[:HEAD, :]
        at = pl.multiple_of(lax.rem(y + 2, 4) * HEAD + side * half, half)
        wo_ref[pl.ds(at, half), :] = ref[HEAD:, :]
    tokens, used = row_of((x0, x1, x2, x3))
    far = jnp.concatenate(heads(tokens, used, w_ref), axis=0)
    wo_a = wo_ref[pl.ds(pl.multiple_of(core * LANES, LANES), LANES), :]
    wo_b = wo_ref[pl.ds(pl.multiple_of((1 - core) * LANES, LANES), LANES), :]
    part = jnp.dot(near_ref[...], wo_a, preferred_element_type=jnp.float32)
    part = part + jnp.dot(far, wo_b, preferred_element_type=jnp.float32)
    for c in range(4):
        part_ref[lax.rem(x + c, 4)] = part[c * length : (c + 1) * length].astype(jnp.bfloat16)


def embed_kernel(weight_ref, parts_ref, x_ref, out_ref, ext_ref, row_ref):
    rows, width = x_ref.shape[1:]
    mixed = x_ref[0].astype(jnp.float32)
    for n in range(4):
        mixed = mixed + parts_ref[n].astype(jnp.float32)
    centred = mixed - jnp.mean(mixed, axis=1, keepdims=True)
    squares = jnp.sum(centred * centred, axis=1, keepdims=True)
    embedded = (centred / jnp.sqrt(squares + 0.001)).astype(jnp.bfloat16)
    out_ref[0] = embedded
    tail = jnp.concatenate(
        [jnp.broadcast_to(weight_ref[...].astype(jnp.float32), (PAD, LANES)), jnp.zeros((PAD, width - LANES), jnp.float32)],
        axis=1,
    ).astype(jnp.bfloat16)
    ext_ref[:rows, :] = embedded
    ext_ref[rows:, :] = tail
    for n in range(4):
        row_ref[n, :rows, :] = embedded
        row_ref[n, rows:, :] = tail


def pairs_kernel(row_ref, near_ref, far_ref, own_ref, out_ref):
    x = lax.axis_index("x")
    y = lax.axis_index("y")
    n = LANES
    me = x * 4 + y
    near = x * 4 + lax.rem(y + 1, 4)
    far = x * 4 + lax.rem(y + 2, 4)
    has_far = jnp.logical_or(y == 0, y == 3)
    rows = jnp.concatenate([row_ref[c, :n, :] for c in range(4)], axis=0)
    cols = jnp.concatenate([near_ref[:n, :], far_ref[:n, :], own_ref[:n, :]], axis=0)
    similar = lax.dot_general(rows, cols, (((1,), (1,)), ((), ())), preferred_element_type=jnp.float32)
    col_weight = [r[n : n + 1, :n].astype(jnp.float32) for r in (near_ref, far_ref, own_ref)]
    row_weight = [row_ref[c, n : n + 1, :n].astype(jnp.float32) for c in range(4)]
    down = [jnp.transpose(jnp.broadcast_to(w, (n, n))) for w in row_weight]
    row_sum = [jnp.sum(w, axis=1, keepdims=True) for w in row_weight]
    col_sum = [jnp.sum(w, axis=1, keepdims=True) for w in col_weight]
    col_sum[1] = jnp.where(has_far, col_sum[1], 1.0)
    dest = lax.broadcasted_iota(jnp.int32, (16, LANES), 0)
    lane = lax.broadcasted_iota(jnp.int32, (16, LANES), 1)
    total = jnp.zeros((16, LANES), jnp.float32)
    for j, other in enumerate((near, far, me)):
        w_col = col_weight[j]
        for c in range(4):
            block = similar[c * n : (c + 1) * n, j * n : (j + 1) * n]
            best_col = jnp.max(jnp.where(w_col > 0, block, -4.0), axis=1, keepdims=True)
            best_row = jnp.max(jnp.where(down[c] > 0, block, -4.0), axis=0, keepdims=True)
            forward = jnp.sum(best_col * down[c][:, :1], axis=0, keepdims=True) / row_sum[c]
            backward = jnp.sum(best_row * w_col, axis=1, keepdims=True) / col_sum[j]
            utility = 0.5 * (forward + backward)
            mate = c * 4 + y
            here = jnp.logical_and(dest == other, lane == mate)
            if j < 2:
                here = jnp.logical_or(here, jnp.logical_and(dest == mate, lane == other))
            if j == 1:
                here = jnp.logical_and(here, has_far)
            total = total + jnp.where(here, jnp.broadcast_to(utility, total.shape), 0.0)
    for p in range(16):
        out_ref[p] = jnp.broadcast_to(total[p : p + 1], (8, LANES))


def finish_kernel(got_ref, pair_ref, mean_ref):
    me = lax.axis_index("x") * 4 + lax.axis_index("y")
    total = got_ref[0]
    for p in range(1, 16):
        total = total + got_ref[p]
    lane = lax.broadcasted_iota(jnp.int32, total.shape, 1)
    pair_ref[...] = total[:1, :16]
    rest = jnp.where(jnp.logical_and(lane < 16, lane != me), total, 0.0)
    mean_ref[...] = (jnp.sum(rest, axis=1, keepdims=True) / 15)[:1]


def call(kernel, ins, outs, *args, scratch=(), mebibytes=20):
    return pl.pallas_call(
        kernel,
        in_specs=ins,
        out_specs=tuple(VMEM for _ in outs) if len(outs) > 1 else VMEM,
        out_shape=outs if len(outs) > 1 else outs[0],
        scratch_shapes=list(scratch),
        compiler_params=params(mebibytes),
    )(*args)


def shift(size, by):
    return [((i + by) % size, i) for i in range(size)]


def sideways():
    pairs = []
    for y in range(8):
        for core in range(2):
            source = (y + (1 if core == 0 else 7)) % 8
            pairs.append(((source // 4 * 2 + core) * 4 + source % 4, (y // 4 * 2 + core) * 4 + y % 4))
    return pairs


def windows():
    groups = []
    for z in range(8):
        for core in range(2):
            for run in range(2):
                start = 4 * run + 2 * core + z % 2
                ys = sorted(((start + i) % 8 for i in range(4)), key=lambda y: y % 4)
                groups.append(
                    [(((y // 4 * 8 + z) * 2 + core) * 4 + x) * 4 + y % 4 for x in range(4) for y in ys]
                )
    return groups


def spread(chunks):
    axes = ("yh", "z", "core", "x", "y")
    return lax.all_to_all(chunks, axes, split_axis=0, concat_axis=0, tiled=True, axis_index_groups=windows())


def shards(layer_input, token_ids, lengths, idf_table, query_weight, key_weight, value_weight, output_weight):
    _, length, width = layer_input.shape
    depth = query_weight.shape[0]
    bf16, f32 = jnp.bfloat16, jnp.float32
    hbm = pl.BlockSpec(memory_space=pltpu.HBM)
    chunks = pl.pallas_call(
        chunks_kernel,
        in_specs=[hbm] * 3,
        out_specs=hbm,
        out_shape=jax.ShapeDtypeStruct((16, depth, 3 * LANES), bf16),
        scratch_shapes=[
            pltpu.VMEM((4, depth, 3 * LANES), bf16),
            pltpu.SemaphoreType.DMA((12,)),
            pltpu.SemaphoreType.DMA((16,)),
        ],
        compiler_params=params(63),
    )(query_weight, key_weight, value_weight)
    used = jnp.broadcast_to(lengths.astype(f32)[:, None], (1, LANES))
    extended, half, block = call(
        extend_kernel,
        [VMEM] * 3,
        (
            jax.ShapeDtypeStruct((length + PAD, width), bf16),
            jax.ShapeDtypeStruct((depth // 2, width), bf16),
            jax.ShapeDtypeStruct((depth, width), bf16),
        ),
        layer_input, used, output_weight,
    )
    beside = lax.ppermute(block, ("yh", "core", "y"), sideways())
    across = lax.ppermute(half, ("yh", "y"), shift(8, 2))
    weights = spread(chunks)
    others = [lax.ppermute(extended, "x", shift(4, k)) for k in (1, 2, 3)]
    mine = jnp.concatenate([beside, across], axis=0)
    positions = jnp.arange(length, dtype=jnp.int32)
    valid = positions[None, :] < lengths[:, None]
    token_weight = (jnp.take(idf_table, token_ids, axis=0) * valid.astype(f32)).astype(bf16)
    weights, others, token_weight, mine = lax.optimization_barrier((weights, others, token_weight, mine))
    near_half = weights.reshape(width, 3 * LANES)
    far_half = lax.ppermute(near_half, "core", [(0, 1), (1, 0)])
    mate = lax.ppermute(mine, "core", [(0, 1), (1, 0)])
    context = call(
        near_kernel, [VMEM] * 5, (jax.ShapeDtypeStruct((4 * length, 2 * HEAD), bf16),), extended, *others, near_half
    )
    parts = call(
        far_kernel,
        [VMEM] * 9,
        (jax.ShapeDtypeStruct((4, length, width), bf16),),
        extended, *others, far_half, context, output_weight, mine, mate,
        scratch=(pltpu.VMEM((4 * HEAD, width), bf16),),
    )
    parts = lax.all_to_all(parts, "x", split_axis=0, concat_axis=0, tiled=True)
    embedded, own, row = call(
        embed_kernel,
        [VMEM] * 3,
        (
            jax.ShapeDtypeStruct((1, length, width), bf16),
            jax.ShapeDtypeStruct((length + PAD, width), bf16),
            jax.ShapeDtypeStruct((4, length + PAD, width), bf16),
        ),
        token_weight, parts, layer_input,
    )
    near = lax.ppermute(own, "y", shift(4, 1))
    far = lax.ppermute(own, "y", [(2, 0), (1, 3)])
    row = lax.all_to_all(row, "x", split_axis=0, concat_axis=0, tiled=True)
    known = call(
        pairs_kernel, [VMEM] * 4, (jax.ShapeDtypeStruct((16, 8, LANES), f32),), row, near, far, own
    )
    known = lax.all_to_all(known, ("x", "y"), split_axis=0, concat_axis=0, tiled=True)
    pair, mean = call(
        finish_kernel,
        [VMEM],
        (jax.ShapeDtypeStruct((1, 16), f32), jax.ShapeDtypeStruct((1, 1), f32)),
        known,
    )
    return embedded, pair, mean.reshape(1)


def solution(mesh):
    fine = Mesh(np.asarray(mesh.devices).reshape(2, 8, 2, 4, 4), ("yh", "z", "core", "x", "y"))
    src = ("yh", "z", "core")
    cand = ("x", "y")
    in_specs = (
        P(src + cand, None, None),
        P(src + cand, None),
        P(src + cand),
        P(src),
        P(cand, None),
        P(cand, None),
        P(cand, None),
        P(cand, None),
    )
    out_specs = (P(src + cand, None, None), P(src + cand, None), P(src + cand))
    return jax.shard_map(shards, mesh=fine, in_specs=in_specs, out_specs=out_specs, check_vma=False)
```

```python
import functools

import jax
import jax.numpy as jnp
import numpy as np
from jax import lax
from jax.experimental import pallas as pl
from jax.experimental.pallas import tpu as pltpu
from jax.sharding import Mesh, PartitionSpec as P

HEAD = 64
LANES = 128
PAD = 16
VMEM = pl.BlockSpec(memory_space=pltpu.VMEM)
SMEM = pl.BlockSpec(memory_space=pltpu.SMEM)


def params(mebibytes):
    return pltpu.CompilerParams(vmem_limit_bytes=mebibytes * 1024 * 1024)


def chunks_kernel(q_hbm, k_hbm, v_hbm, chunk_hbm, piece_ref, sems, out_sems):
    core = lax.axis_index("core")
    copies = []
    for block in range(4):
        at = pl.multiple_of(block * 2 * LANES + core * LANES, LANES)
        for n, ref in enumerate((q_hbm, k_hbm, v_hbm)):
            to = piece_ref.at[block, :, pl.ds(n * LANES, LANES)]
            copies.append(pltpu.make_async_copy(ref.at[:, pl.ds(at, LANES)], to, sems.at[block * 3 + n]))
    for copy in copies:
        copy.start()
    sends = []
    for block in range(4):
        for n in range(3):
            copies[block * 3 + n].wait()
        for y in range(4):
            p = block * 4 + y
            send = pltpu.make_async_copy(piece_ref.at[block], chunk_hbm.at[p], out_sems.at[p])
            send.start()
            sends.append(send)
    for send in sends:
        send.wait()


def extend_kernel(x_ref, used_ref, o_ref, ext_ref, half_ref, block_ref):
    half = half_ref.shape[0]
    block_ref[...] = o_ref[...]
    half_ref[...] = o_ref[pl.ds(pl.multiple_of(lax.axis_index("core") * half, half), half), :]
    rows = x_ref.shape[1]
    ext_ref[:rows, :] = x_ref[0]
    used = jnp.concatenate([used_ref[...]] * (ext_ref.shape[1] // LANES), axis=1)
    ext_ref[rows:, :] = jnp.broadcast_to(used, (PAD, ext_ref.shape[1])).astype(jnp.bfloat16)


def heads(tokens, used, w_ref):
    length = LANES
    first = lax.broadcasted_iota(jnp.int32, (length, LANES), 1) < HEAD
    position = lax.broadcasted_iota(jnp.int32, (2 * length, length), 1).astype(jnp.float32)
    qkv = jnp.dot(tokens, w_ref[...], preferred_element_type=jnp.float32).astype(jnp.bfloat16)
    out = []
    for c in range(4):
        rows = slice(c * length, (c + 1) * length)
        q = qkv[rows, :LANES]
        key = qkv[rows, LANES : 2 * LANES]
        v = qkv[rows, 2 * LANES :]
        zero = jnp.zeros_like(q)
        both = jnp.concatenate([jnp.where(first, q, zero), jnp.where(first, zero, q)], axis=0)
        scores = lax.dot_general(
            both, key, (((1,), (1,)), ((), ())), preferred_element_type=jnp.float32
        ) * (HEAD ** -0.5)
        scores = jnp.where(position < used[c], scores, -1e9)
        expo = jnp.exp(scores - jnp.max(scores, axis=1, keepdims=True))
        probs = (expo / jnp.sum(expo, axis=1, keepdims=True)).astype(jnp.bfloat16)
        ctx = jnp.dot(probs, v, preferred_element_type=jnp.float32)
        out.append(jnp.where(first, ctx[:length], ctx[length:]).astype(jnp.bfloat16))
    return out


def row_of(refs):
    length = LANES
    tokens = jnp.concatenate([r[:length, :] for r in refs], axis=0)
    return tokens, [r[length : length + 1, :length].astype(jnp.float32) for r in refs]


def near_kernel(x0, x1, x2, x3, w_ref, out_ref):
    tokens, used = row_of((x0, x1, x2, x3))
    for c, context in enumerate(heads(tokens, used, w_ref)):
        out_ref[c * LANES : (c + 1) * LANES, :] = context


def far_kernel(x0, x1, x2, x3, w_ref, near_ref, own_ref, mine_ref, mate_ref, part_ref, wo_ref):
    core = lax.axis_index("core")
    x = lax.axis_index("x")
    y = lax.axis_index("y")
    length = LANES
    half = HEAD // 2
    wo_ref[pl.ds(pl.multiple_of(y * HEAD, HEAD), HEAD), :] = own_ref[...]
    for side, ref in ((core, mine_ref), (1 - core, mate_ref)):
        at = pl.multiple_of(lax.rem(y + 1 + 2 * side, 4) * HEAD, HEAD)
        wo_ref[pl.ds(at, HEAD), :] = ref[:HEAD, :]
        at = pl.multiple_of(lax.rem(y + 2, 4) * HEAD + side * half, half)
        wo_ref[pl.ds(at, half), :] = ref[HEAD:, :]
    tokens, used = row_of((x0, x1, x2, x3))
    far = jnp.concatenate(heads(tokens, used, w_ref), axis=0)
    wo_a = wo_ref[pl.ds(pl.multiple_of(core * LANES, LANES), LANES), :]
    wo_b = wo_ref[pl.ds(pl.multiple_of((1 - core) * LANES, LANES), LANES), :]
    part = jnp.dot(near_ref[...], wo_a, preferred_element_type=jnp.float32)
    part = part + jnp.dot(far, wo_b, preferred_element_type=jnp.float32)
    for c in range(4):
        part_ref[lax.rem(x + c, 4)] = part[c * length : (c + 1) * length].astype(jnp.bfloat16)


def embed_kernel(weight_ref, parts_ref, x_ref, out_ref, ext_ref, row_ref):
    rows, width = x_ref.shape[1:]
    mixed = x_ref[0].astype(jnp.float32)
    for n in range(4):
        mixed = mixed + parts_ref[n].astype(jnp.float32)
    centred = mixed - jnp.mean(mixed, axis=1, keepdims=True)
    squares = jnp.sum(centred * centred, axis=1, keepdims=True)
    embedded = (centred / jnp.sqrt(squares + 0.001)).astype(jnp.bfloat16)
    out_ref[0] = embedded
    tail = jnp.concatenate(
        [jnp.broadcast_to(weight_ref[...].astype(jnp.float32), (PAD, LANES)), jnp.zeros((PAD, width - LANES), jnp.float32)],
        axis=1,
    ).astype(jnp.bfloat16)
    ext_ref[:rows, :] = embedded
    ext_ref[rows:, :] = tail
    for n in range(4):
        row_ref[n, :rows, :] = embedded
        row_ref[n, rows:, :] = tail


def pairs_kernel(row_ref, near_ref, far_ref, own_ref, out_ref):
    x = lax.axis_index("x")
    y = lax.axis_index("y")
    n = LANES
    me = x * 4 + y
    near = x * 4 + lax.rem(y + 1, 4)
    far = x * 4 + lax.rem(y + 2, 4)
    has_far = jnp.logical_or(y == 0, y == 3)
    rows = jnp.concatenate([row_ref[c, :n, :] for c in range(4)], axis=0)
    cols = jnp.concatenate([near_ref[:n, :], far_ref[:n, :], own_ref[:n, :]], axis=0)
    similar = lax.dot_general(rows, cols, (((1,), (1,)), ((), ())), preferred_element_type=jnp.float32)
    col_weight = [r[n : n + 1, :n].astype(jnp.float32) for r in (near_ref, far_ref, own_ref)]
    row_weight = [row_ref[c, n : n + 1, :n].astype(jnp.float32) for c in range(4)]
    down = [jnp.transpose(jnp.broadcast_to(w, (n, n))) for w in row_weight]
    row_sum = [jnp.sum(w, axis=1, keepdims=True) for w in row_weight]
    col_sum = [jnp.sum(w, axis=1, keepdims=True) for w in col_weight]
    col_sum[1] = jnp.where(has_far, col_sum[1], 1.0)
    dest = lax.broadcasted_iota(jnp.int32, (16, LANES), 0)
    lane = lax.broadcasted_iota(jnp.int32, (16, LANES), 1)
    total = jnp.zeros((16, LANES), jnp.float32)
    for j, other in enumerate((near, far, me)):
        w_col = col_weight[j]
        for c in range(4):
            block = similar[c * n : (c + 1) * n, j * n : (j + 1) * n]
            best_col = jnp.max(jnp.where(w_col > 0, block, -4.0), axis=1, keepdims=True)
            best_row = jnp.max(jnp.where(down[c] > 0, block, -4.0), axis=0, keepdims=True)
            forward = jnp.sum(best_col * down[c][:, :1], axis=0, keepdims=True) / row_sum[c]
            backward = jnp.sum(best_row * w_col, axis=1, keepdims=True) / col_sum[j]
            utility = 0.5 * (forward + backward)
            mate = c * 4 + y
            here = jnp.logical_and(dest == other, lane == mate)
            if j < 2:
                here = jnp.logical_or(here, jnp.logical_and(dest == mate, lane == other))
            if j == 1:
                here = jnp.logical_and(here, has_far)
            total = total + jnp.where(here, jnp.broadcast_to(utility, total.shape), 0.0)
    for p in range(16):
        out_ref[p] = total[p : p + 1]


def finish_kernel(got_ref, pair_ref, mean_ref):
    me = lax.axis_index("x") * 4 + lax.axis_index("y")
    total = got_ref[0]
    for p in range(1, 16):
        total = total + got_ref[p]
    lane = lax.broadcasted_iota(jnp.int32, total.shape, 1)
    pair_ref[...] = total[:1, :16]
    rest = jnp.where(jnp.logical_and(lane < 16, lane != me), total, 0.0)
    mean_ref[...] = (jnp.sum(rest, axis=1, keepdims=True) / 15)[:1]


def call(kernel, ins, outs, *args, scratch=(), mebibytes=20):
    return pl.pallas_call(
        kernel,
        in_specs=ins,
        out_specs=tuple(VMEM for _ in outs) if len(outs) > 1 else VMEM,
        out_shape=outs if len(outs) > 1 else outs[0],
        scratch_shapes=list(scratch),
        compiler_params=params(mebibytes),
    )(*args)


def shift(size, by):
    return [((i + by) % size, i) for i in range(size)]


def sideways():
    pairs = []
    for y in range(8):
        for core in range(2):
            source = (y + (1 if core == 0 else 7)) % 8
            pairs.append(((source // 4 * 2 + core) * 4 + source % 4, (y // 4 * 2 + core) * 4 + y % 4))
    return pairs


def windows():
    groups = []
    for z in range(8):
        for core in range(2):
            for run in range(2):
                start = 4 * run + 2 * core + z % 2
                ys = sorted(((start + i) % 8 for i in range(4)), key=lambda y: y % 4)
                groups.append(
                    [(((y // 4 * 8 + z) * 2 + core) * 4 + x) * 4 + y % 4 for x in range(4) for y in ys]
                )
    return groups


def spread(chunks):
    axes = ("yh", "z", "core", "x", "y")
    return lax.all_to_all(chunks, axes, split_axis=0, concat_axis=0, tiled=True, axis_index_groups=windows())


def shards(layer_input, token_ids, lengths, idf_table, query_weight, key_weight, value_weight, output_weight):
    _, length, width = layer_input.shape
    depth = query_weight.shape[0]
    bf16, f32 = jnp.bfloat16, jnp.float32
    hbm = pl.BlockSpec(memory_space=pltpu.HBM)
    chunks = pl.pallas_call(
        chunks_kernel,
        in_specs=[hbm] * 3,
        out_specs=hbm,
        out_shape=jax.ShapeDtypeStruct((16, depth, 3 * LANES), bf16),
        scratch_shapes=[
            pltpu.VMEM((4, depth, 3 * LANES), bf16),
            pltpu.SemaphoreType.DMA((12,)),
            pltpu.SemaphoreType.DMA((16,)),
        ],
        compiler_params=params(63),
    )(query_weight, key_weight, value_weight)
    used = jnp.broadcast_to(lengths.astype(f32)[:, None], (1, LANES))
    extended, half, block = call(
        extend_kernel,
        [VMEM] * 3,
        (
            jax.ShapeDtypeStruct((length + PAD, width), bf16),
            jax.ShapeDtypeStruct((depth // 2, width), bf16),
            jax.ShapeDtypeStruct((depth, width), bf16),
        ),
        layer_input, used, output_weight,
    )
    beside = lax.ppermute(block, ("yh", "core", "y"), sideways())
    across = lax.ppermute(half, ("yh", "y"), shift(8, 2))
    weights = spread(chunks)
    others = [lax.ppermute(extended, "x", shift(4, k)) for k in (1, 2, 3)]
    mine = jnp.concatenate([beside, across], axis=0)
    positions = jnp.arange(length, dtype=jnp.int32)
    valid = positions[None, :] < lengths[:, None]
    token_weight = (jnp.take(idf_table, token_ids, axis=0) * valid.astype(f32)).astype(bf16)
    weights, others, token_weight, mine = lax.optimization_barrier((weights, others, token_weight, mine))
    near_half = weights.reshape(width, 3 * LANES)
    far_half = lax.ppermute(near_half, "core", [(0, 1), (1, 0)])
    mate = lax.ppermute(mine, "core", [(0, 1), (1, 0)])
    context = call(
        near_kernel, [VMEM] * 5, (jax.ShapeDtypeStruct((4 * length, 2 * HEAD), bf16),), extended, *others, near_half
    )
    parts = call(
        far_kernel,
        [VMEM] * 9,
        (jax.ShapeDtypeStruct((4, length, width), bf16),),
        extended, *others, far_half, context, output_weight, mine, mate,
        scratch=(pltpu.VMEM((4 * HEAD, width), bf16),),
    )
    parts = lax.all_to_all(parts, "x", split_axis=0, concat_axis=0, tiled=True)
    embedded, own, row = call(
        embed_kernel,
        [VMEM] * 3,
        (
            jax.ShapeDtypeStruct((1, length, width), bf16),
            jax.ShapeDtypeStruct((length + PAD, width), bf16),
            jax.ShapeDtypeStruct((4, length + PAD, width), bf16),
        ),
        token_weight, parts, layer_input,
    )
    near = lax.ppermute(own, "y", shift(4, 1))
    far = lax.ppermute(own, "y", [(2, 0), (1, 3)])
    row = lax.all_to_all(row, "x", split_axis=0, concat_axis=0, tiled=True)
    known = call(
        pairs_kernel, [VMEM] * 4, (jax.ShapeDtypeStruct((16, 1, LANES), f32),), row, near, far, own
    )
    known = lax.all_to_all(known, ("x", "y"), split_axis=0, concat_axis=0, tiled=True)
    pair, mean = call(
        finish_kernel,
        [VMEM],
        (jax.ShapeDtypeStruct((1, 16), f32), jax.ShapeDtypeStruct((1, 1), f32)),
        known,
    )
    return embedded, pair, mean.reshape(1)


def solution(mesh):
    fine = Mesh(np.asarray(mesh.devices).reshape(2, 8, 2, 4, 4), ("yh", "z", "core", "x", "y"))
    src = ("yh", "z", "core")
    cand = ("x", "y")
    in_specs = (
        P(src + cand, None, None),
        P(src + cand, None),
        P(src + cand),
        P(src),
        P(cand, None),
        P(cand, None),
        P(cand, None),
        P(cand, None),
    )
    out_specs = (P(src + cand, None, None), P(src + cand, None), P(src + cand))
    return jax.shard_map(shards, mesh=fine, in_specs=in_specs, out_specs=out_specs, check_vma=False)
```
